128 devices in a mesh: dp: 16 (over x, y), seq: 8 (over z, core).
Axes of the slice: x: 4, y: 4, z: 4, core: 2. Of those that a mesh axis runs over, the one named last changes fastest.
Arguments:
- tokens: bfloat16 [32768, 1280], P(('dp', 'seq')), may hold values from -8 to 8
- norm_gain: float32 [1280], replicated, may hold values from 0.1 to 1.9
- w_qkv: bfloat16 [1280, 3840], replicated, may hold values from -1.5 to 1.5
- w_out: bfloat16 [1280, 1280], replicated, may hold values from -0.15625 to 0.15625
- cotangent: bfloat16 [32768, 1280], P(('dp', 'seq')), may hold values from -6 to 6
- segment: int32 [32768], P(('dp', 'seq')), may hold values from 0 to 63, as said below
- patch_row: int32 [32768], P(('dp', 'seq')), may hold values from 0 to 249, as said below
- patch_col: int32 [32768], P(('dp', 'seq')), may hold values from 0 to 15, as said below
Outputs:
- result: bfloat16 [32768, 1280], P(('dp', 'seq'))
- grad_tokens: bfloat16 [32768, 1280], P(('dp', 'seq'))
- grad_qkv: float32 [1280, 3840], P(('dp', 'seq'))
- grad_out: float32 [1280, 1280], P(('dp', 'seq'))
- grad_gain: float32 [1280], P(('dp', 'seq'))
The draws below stay inside these ranges and needn't reach their ends.
Inputs may be any that keep to these rules, and one draw needn't show every extreme that they name: `segment`: each batch of 2048 patches (one index of dp) holds 4 images in order; image k of batch a is numbered a * 4 + k and has a positive multiple of 16 patches. `patch_row`: an image's patches run row by row, 8 or 16 to a row. `patch_col`: column within the row, below the image's row width.
All inputs are finite; a program needn't handle non-finite values.
Results may differ from the reference program's by a relative error of at most 0.014.
Values may be sent and summed in bfloat16 or wider, within the bound.
No kernel may reach another device: no remote copies, remote signals or barrier semaphores. Data moves between devices by JAX's collectives and lax.ppermute only.
A program may use at most 192 MiB of HBM per device.

```python
import jax
import jax.numpy as jnp
from jax import lax

D = 1280
HEADS = 16
NIMG = 4
SEQ_LEN = 2048
TOKENS = 32768
N_DP = 16


def image_layout(key):
    group_keys = jax.random.split(key, N_DP)
    group_index = jnp.arange(N_DP, dtype=jnp.int32)

    def one_group(group_key, group_number):
        key_cuts, key_width = jax.random.split(group_key)
        unit_count = SEQ_LEN // 16
        cut_points = jnp.sort(jax.random.permutation(key_cuts, unit_count - 1)[:NIMG - 1] + 1).astype(jnp.int32)
        fixed_cuts = (unit_count - NIMG + jnp.arange(1, NIMG, dtype=jnp.int32)).astype(jnp.int32)
        first_group = group_number == 0
        cut_points = jnp.where(first_group, fixed_cuts, cut_points)
        bounds = jnp.concatenate([jnp.zeros((1,), jnp.int32), cut_points, jnp.full((1,), unit_count, jnp.int32)]) * 16
        widths = 8 * (1 + jax.random.randint(key_width, (NIMG,), 0, 2)).astype(jnp.int32)
        fixed_widths = jnp.where(jnp.arange(NIMG, dtype=jnp.int32) == 0, 8, 16).astype(jnp.int32)
        widths = jnp.where(first_group, fixed_widths, widths)
        position = jnp.arange(SEQ_LEN, dtype=jnp.int32)
        image_of = jnp.sum((position[:, None] >= bounds[None, 1:NIMG]).astype(jnp.int32), axis=1).astype(jnp.int32)
        start_at = bounds[image_of]
        row_width = widths[image_of]
        local_idx = position - start_at
        return (image_of, local_idx // row_width, local_idx % row_width)
    image_of, row_of, col_of = jax.vmap(one_group)(group_keys, group_index)
    image_of = image_of + jnp.arange(N_DP, dtype=jnp.int32)[:, None] * NIMG
    return (image_of.reshape(-1), row_of.reshape(-1), col_of.reshape(-1))


def draw_segment(key, part):
    return image_layout(key)[0]


def draw_patch_row(key, part):
    return image_layout(key)[1]


def draw_patch_col(key, part):
    return image_layout(key)[2]


def draw_tokens(key, part):
    key = jax.random.fold_in(key, 11)
    base_draw = jnp.clip(jax.random.normal(key, (TOKENS, D), jnp.float32), -6.0, 6.0)
    return base_draw.astype(jnp.bfloat16)


def draw_w_qkv(key, part):
    key = jax.random.fold_in(key, 23)
    key_base = jax.random.fold_in(key, 0)
    base_draw = jnp.clip(jax.random.normal(key_base, (D, 3 * D), jnp.float32), -6.0, 6.0) * D ** (-0.5)
    return base_draw.astype(jnp.bfloat16)


def block_levels(stream_key, extent, shards, smallest, largest):
    gain, own = 1.0, jax.random.fold_in(stream_key, 6)
    for axis_at, shards_of in shards:
        steps = jnp.exp(jax.random.uniform(jax.random.fold_in(own, axis_at), (shards_of,), jnp.float32, smallest / len(shards), largest / len(shards)))
        gain = gain * jnp.repeat(steps, extent[axis_at] // shards_of).reshape([-1 if axis == axis_at else 1 for axis in range(len(extent))])
    return gain


def centred(own_key, extent, scale, limit, shards=(), kind=jnp.bfloat16):
    gain = block_levels(own_key, extent, shards, -0.22, 0.18) if shards else 1.0
    values = jax.random.normal(own_key, extent, jnp.float32) * scale * gain
    return jnp.minimum(jnp.maximum(values, -limit), limit).astype(kind)


def setup_inputs(seed: int = 0) -> dict:
    seeds = jax.random.split(jax.random.key(seed), 9)
    tokens = draw_tokens(jax.random.fold_in(seeds[8], 71), 0)
    norm_gain = jnp.clip(1.0 + 0.18 * jax.random.normal(seeds[1], (D,), jnp.float32), 0.1, 1.9)
    w_qkv = draw_w_qkv(jax.random.fold_in(seeds[8], 71), 0)
    w_out = centred(seeds[3], (D, D), D ** -0.5, 0.15625)
    cotangent = centred(seeds[4], (TOKENS, D), 1.0, 6.0, ((0, 128),))
    segment = draw_segment(jax.random.fold_in(seeds[8], 71), 0)
    patch_row = draw_patch_row(jax.random.fold_in(seeds[8], 71), 0)
    patch_col = draw_patch_col(jax.random.fold_in(seeds[8], 71), 0)
    return dict(tokens=tokens, norm_gain=norm_gain, w_qkv=w_qkv, w_out=w_out, cotangent=cotangent, segment=segment, patch_row=patch_row, patch_col=patch_col)


NORM_EPSILON = 1e-06
ROPE_BASE = 10000.0

def rope_tables(patch_row, patch_col, head_size):
    quarter = head_size // 4
    frequency = ROPE_BASE ** (-jnp.arange(quarter, dtype=jnp.float32) / quarter)
    angles = jnp.concatenate([patch_row.astype(jnp.float32)[:, None] * frequency, patch_col.astype(jnp.float32)[:, None] * frequency], axis=1)
    angles = jnp.concatenate([angles, angles], axis=1)
    return (jnp.cos(angles), jnp.sin(angles))

def rotate(values, cos_table, sin_table):
    half_size = values.shape[-1] // 2
    turned = jnp.concatenate([-values[..., half_size:], values[..., :half_size]], axis=-1)
    return values * cos_table[:, None, :] + turned * sin_table[:, None, :]

def attend_group(stacked, image_of, score_scale):
    query = stacked[:, 0].astype(jnp.float32)
    key_rows = stacked[:, 1].astype(jnp.float32)
    values = stacked[:, 2].astype(jnp.float32)
    grad_mixed = stacked[:, 3].astype(jnp.float32)
    scores = jnp.einsum('qhd,khd->hqk', query, key_rows) * score_scale
    same_image = image_of[:, None] == image_of[None, :]
    scores = jnp.where(same_image[None], scores, -jnp.inf)
    row_top = lax.optimization_barrier(jnp.max(scores, axis=-1, keepdims=True))
    exponent = jnp.exp(scores - row_top)
    attn_probs = (exponent / lax.optimization_barrier(jnp.sum(exponent, axis=-1, keepdims=True))).astype(jnp.bfloat16)
    prob_wide = attn_probs.astype(jnp.float32)
    mixed_out = jnp.einsum('hqk,khd->qhd', prob_wide, values).astype(jnp.bfloat16)
    grad_prob = jnp.einsum('qhd,khd->hqk', grad_mixed, values)
    centre = lax.optimization_barrier(jnp.sum(prob_wide * grad_prob, axis=-1, keepdims=True))
    grad_score = (prob_wide * (grad_prob - centre) * score_scale).astype(jnp.bfloat16).astype(jnp.float32)
    grad_query = jnp.einsum('hqk,khd->qhd', grad_score, key_rows).astype(jnp.bfloat16)
    grad_key = jnp.einsum('hqk,qhd->khd', grad_score, query).astype(jnp.bfloat16)
    grad_value = jnp.einsum('hqk,qhd->khd', prob_wide, grad_mixed).astype(jnp.bfloat16)
    return jnp.stack([mixed_out, grad_query, grad_key, grad_value], axis=1)

def reference(tokens, norm_gain, w_qkv, w_out, cotangent, segment, patch_row, patch_col):
    head_size = D // HEADS
    score_scale = float(head_size) ** (-0.5)
    tok_wide = tokens.astype(jnp.float32)
    inverse_rms = lax.rsqrt(lax.optimization_barrier(jnp.mean(tok_wide * tok_wide, axis=-1, keepdims=True)) + NORM_EPSILON)
    normed = (tok_wide * inverse_rms * norm_gain).astype(jnp.bfloat16)
    qkv_rows = jnp.dot(normed, w_qkv, preferred_element_type=jnp.float32).reshape(TOKENS, 3, HEADS, head_size)
    cos_table, sin_table = rope_tables(patch_row, patch_col, head_size)
    query = rotate(qkv_rows[:, 0], cos_table, sin_table).astype(jnp.bfloat16)
    key_rows = rotate(qkv_rows[:, 1], cos_table, sin_table).astype(jnp.bfloat16)
    values = qkv_rows[:, 2].astype(jnp.bfloat16)
    grad_mixed = jnp.dot(cotangent, w_out.T, preferred_element_type=jnp.float32).astype(jnp.bfloat16)
    grad_mixed = grad_mixed.reshape(TOKENS, HEADS, head_size)
    packed = jnp.stack([query, key_rows, values, grad_mixed], axis=1).reshape(N_DP, SEQ_LEN, 4, HEADS, head_size)
    image_groups = segment.reshape(N_DP, SEQ_LEN)
    returned = lax.map(lambda pair: attend_group(pair[0], pair[1], score_scale), (packed, image_groups))
    returned = returned.reshape(TOKENS, 4, HEADS, head_size)
    mixed_out = returned[:, 0].reshape(TOKENS, D)
    result = (tok_wide + jnp.dot(mixed_out, w_out, preferred_element_type=jnp.float32)).astype(jnp.bfloat16)
    grad_query = rotate(returned[:, 1].astype(jnp.float32), cos_table, -sin_table).astype(jnp.bfloat16)
    grad_key = rotate(returned[:, 2].astype(jnp.float32), cos_table, -sin_table).astype(jnp.bfloat16)
    grad_qkv_rows = jnp.stack([grad_query, grad_key, returned[:, 3]], axis=1).reshape(TOKENS, 3 * D)
    grad_normed = jnp.dot(grad_qkv_rows, w_qkv.T, preferred_element_type=jnp.float32)
    pre_gain = grad_normed * norm_gain
    grad_x = inverse_rms * pre_gain - inverse_rms ** 3 * tok_wide * lax.optimization_barrier(jnp.mean(pre_gain * tok_wide, axis=-1, keepdims=True))
    grad_tokens = (cotangent.astype(jnp.float32) + grad_x).astype(jnp.bfloat16)
    factor = float(TOKENS) ** (-0.5)
    grad_qkv = jnp.dot(normed.T, grad_qkv_rows, preferred_element_type=jnp.float32) * factor
    grad_out = jnp.dot(mixed_out.T, cotangent, preferred_element_type=jnp.float32) * factor
    grad_gain = lax.optimization_barrier(jnp.sum(grad_normed * (tok_wide * inverse_rms), axis=0)) * factor
    return (result, grad_tokens, grad_qkv, grad_out, grad_gain)
```

```python
import functools

import jax
import jax.numpy as jnp
from jax import lax
from jax.experimental import pallas as pl
from jax.experimental.pallas import tpu as pltpu
from jax.sharding import PartitionSpec as P

HEADS = 16
NORM_EPSILON = 1e-06
ROPE_BASE = 10000.0
LOG2E = 1.4426950408889634
LANES = 128
HALF = 64
ONE_LANE = 40
BLOCK_Q = 512
ROW_LIMIT = 256
COL_LIMIT = 128
EXTRA = 16

bf16 = jnp.bfloat16
f32 = jnp.float32

OFFSETS = ((0, 0), (-1, 0), (1, 0), (2, 0), (0, 1), (-1, 1), (1, 1), (2, 1))
MIRROR = (0, 2, 1, 3, 4, 6, 5, 7)
VMEM = pl.BlockSpec(memory_space=pltpu.VMEM)
SMEM = pl.BlockSpec(memory_space=pltpu.SMEM)


def dot_nt(a, b):
    return lax.dot_general(a, b, (((1,), (1,)), ((), ())), preferred_element_type=f32)


def dot_nn(a, b):
    return lax.dot_general(a, b, (((1,), (0,)), ((), ())), preferred_element_type=f32)


def dot_tn(a, b):
    return lax.dot_general(a, b, (((0,), (0,)), ((), ())), preferred_element_type=f32)


def shift(value, offset, size):
    dz, dc = offset
    depth = size // 2
    pairs = [(i, ((i // 2 + dz) % depth) * 2 + ((i % 2) ^ dc)) for i in range(size)]
    return lax.ppermute(value, "seq", pairs)


def params(mib):
    return pltpu.CompilerParams(vmem_limit_bytes=mib * 2**20)


def cost(flops, nbytes, exps=0):
    return pl.CostEstimate(flops=flops, bytes_accessed=nbytes, transcendentals=exps)


def norm_kernel(tok_ref, gain_ref, seg_ref, row_ref, col_ref, out_ref):
    rows = tok_ref.shape[0]
    wide = tok_ref[...].astype(f32)
    inverse = lax.rsqrt(jnp.mean(wide * wide, axis=-1, keepdims=True) + NORM_EPSILON)
    out_ref[:rows, :] = (wide * inverse * gain_ref[...]).astype(bf16)
    out_ref[rows:, :] = jnp.zeros((EXTRA, out_ref.shape[1]), bf16)
    places = [r[...].astype(f32) for r in (seg_ref, row_ref, col_ref)]
    places.append(jnp.zeros((EXTRA - 3, rows), f32))
    out_ref[rows:, :rows] = jnp.concatenate(places, axis=0).astype(bf16)


def normalise(tokens, gain, segment, patch_row, patch_col):
    rows, width = tokens.shape
    return pl.pallas_call(
        norm_kernel,
        out_shape=jax.ShapeDtypeStruct((rows + EXTRA, width), bf16),
        in_specs=[VMEM] * 5,
        out_specs=VMEM,
        cost_estimate=cost(8 * rows * width, 4 * rows * width),
    )(tokens, gain[None], segment[None], patch_row[None], patch_col[None])


def grad_mixed_kernel(cot_ref, w_ref, out_ref):
    size, part, lanes = out_ref.shape
    grad = dot_nt(cot_ref[...], w_ref[...])
    own = w_ref.shape[0] // size
    for s in range(size):
        pieces = [
            grad[i * part : (i + 1) * part, s * own : (s + 1) * own] for i in range(lanes // own)
        ]
        out_ref[s] = jnp.concatenate(pieces, axis=1).astype(bf16)


def grad_mixed_blocks(cotangent, w_out, size):
    rows, width = cotangent.shape
    return pl.pallas_call(
        grad_mixed_kernel,
        out_shape=jax.ShapeDtypeStruct((size, rows // 4, 4 * width // size), bf16),
        in_specs=[VMEM] * 2,
        out_specs=VMEM,
        compiler_params=params(32),
        cost_estimate=cost(2 * rows * width * width, 2 * width * width),
    )(cotangent, w_out)


def attend_kernel(*refs):
    at_ref = refs[0]
    blocks = refs[1:9]
    gm_ref, w_ref, table_r_ref, table_c_ref, pick_ref, spread_ref = refs[9:15]
    outs = refs[15:23]
    q, k, v, g, kt, vt, dk, dv, mixed_pad, dq_pad, cos_t, sin_t, seg_c, seg_r = refs[23:]
    length, padded = q.shape
    heads = padded // LANES
    rows = length // len(blocks)
    own = pick_ref.shape[1]
    scale = 80.0**-0.5
    lane = lax.broadcasted_iota(jnp.int32, (1, padded), 1) % LANES

    def halves(u):
        return jnp.concatenate(
            [pltpu.roll(u[:, h * LANES : (h + 1) * LANES], HALF, 1) for h in range(heads)], axis=1
        )

    for b, block in enumerate(blocks):
        r = slice(b * rows, (b + 1) * rows)
        places = block[rows:, :rows].astype(f32)
        seg_r[:, r] = places[0:1, :]
        columns = places.T
        seg_c[r, :] = columns[:, 0:1]
        rows_at = lax.broadcasted_iota(jnp.int32, (rows, ROW_LIMIT), 1).astype(f32)
        cols_at = lax.broadcasted_iota(jnp.int32, (rows, COL_LIMIT), 1).astype(f32)
        hot_r = (columns[:, 1:2] == rows_at).astype(bf16)
        hot_c = (columns[:, 2:3] == cols_at).astype(bf16)
        cos_b = jnp.zeros((rows, LANES), f32)
        sin_b = jnp.zeros((rows, LANES), f32)
        for piece in range(3):
            found = dot_nn(hot_r, table_r_ref[piece]) + dot_nn(hot_c, table_c_ref[piece])
            cos_b += found[:, :LANES]
            sin_b += found[:, LANES:]
        cos_t[r, :] = cos_b
        sin_t[r, :] = sin_b
        qkv = dot_nn(block[:rows, :], w_ref[...])
        cos2 = jnp.concatenate([cos_b] * heads, axis=1)
        sin2 = jnp.concatenate([sin_b] * heads, axis=1)
        qu = qkv[:, :padded]
        ku = qkv[:, padded : 2 * padded]
        q[r, :] = ((qu * cos2 + halves(qu) * sin2) * (scale * LOG2E)).astype(bf16)
        k[r, :] = (ku * cos2 + halves(ku) * sin2).astype(bf16)
        v[r, :] = jnp.where(lane == ONE_LANE, 1.0, qkv[:, 2 * padded :]).astype(bf16)
        packed = gm_ref[at_ref[b]]
        part = packed.shape[0]
        for i in range(rows // part):
            piece = packed[:, i * own : (i + 1) * own]
            start = b * rows + i * part
            g[start : start + part, :] = dot_nn(piece, spread_ref[...]).astype(bf16)

    for h in range(heads):
        c = slice(h * LANES, (h + 1) * LANES)
        kt[h] = k[:, c].T
        vt[h] = v[:, c].T
    dk[...] = jnp.zeros_like(dk)
    dv[...] = jnp.zeros_like(dv)
    segk = seg_c[...]

    def turn_back(x, start):
        r = pl.ds(start, x.shape[0])
        return x * cos_t[r, :] - pltpu.roll(x, HALF, 1) * sin_t[r, :]

    def step(i, carry):
        start = pl.multiple_of(i * BLOCK_Q, BLOCK_Q)
        r = pl.ds(start, BLOCK_Q)
        same = segk == seg_r[:, r]
        for h in range(heads):
            c = slice(h * LANES, (h + 1) * LANES)
            qb = q[r, c]
            gb = g[r, c]
            st = jnp.where(same, dot_nt(k[:, c], qb), -jnp.inf)
            top = jnp.max(st, axis=0, keepdims=True)
            e = jnp.exp2(st - top).astype(bf16)
            ot = dot_nn(vt[h], e)
            o = ot.T
            inv_col = 1.0 / o[:, ONE_LANE : ONE_LANE + 1]
            inv_row = 1.0 / ot[ONE_LANE : ONE_LANE + 1, :]
            mixed_pad[r, c] = (o * inv_col).astype(bf16)
            centre = jnp.sum(gb.astype(f32).T * ot, axis=0, keepdims=True) * inv_row
            dst = (e.astype(f32) * (dot_nt(v[:, c], gb) - centre)).astype(bf16)
            dqt = dot_nn(kt[h], dst) * (inv_row * scale)
            dq_pad[r, c] = turn_back(dqt.T, start).astype(bf16)
            dk[h] += dot_nn(dst, (qb.astype(f32) * inv_col).astype(bf16))
            dv[h] += dot_nn(e, (gb.astype(f32) * inv_col).astype(bf16))
        return carry

    lax.fori_loop(0, length // BLOCK_Q, step, 0)

    for b in range(len(blocks)):
        start = b * rows
        r = slice(start, start + rows)
        pick = pick_ref[...]
        dk_pad = [turn_back(dk[h, r, :] * (1 / LOG2E), start).astype(bf16) for h in range(heads)]
        dv_pad = [dv[h, r, :].astype(bf16) for h in range(heads)]
        parts = [
            mixed_pad[r, :],
            dq_pad[r, :],
            jnp.concatenate(dk_pad, axis=1),
            jnp.concatenate(dv_pad, axis=1),
        ]
        outs[b][...] = jnp.concatenate([dot_nn(p, pick) for p in parts], axis=1).astype(bf16)


def attend(at, blocks, gm, w_own, table_r, table_c, pick, spread):
    rows = blocks[0].shape[0] - EXTRA
    length = rows * len(blocks)
    padded, own = pick.shape
    heads = padded // LANES
    return pl.pallas_call(
        attend_kernel,
        out_shape=[jax.ShapeDtypeStruct((rows, 4 * own), bf16) for _ in blocks],
        in_specs=[SMEM] + [VMEM] * (len(blocks) + 6),
        out_specs=[VMEM] * len(blocks),
        scratch_shapes=[pltpu.VMEM((length, padded), bf16) for _ in range(4)]
        + [pltpu.VMEM((heads, LANES, length), bf16) for _ in range(2)]
        + [pltpu.VMEM((heads, length, LANES), f32) for _ in range(2)]
        + [pltpu.VMEM((length, padded), bf16) for _ in range(2)]
        + [pltpu.VMEM((length, LANES), f32) for _ in range(2)]
        + [pltpu.VMEM((length, 1), f32), pltpu.VMEM((1, length), f32)],
        compiler_params=params(58),
        cost_estimate=cost(
            12 * heads * length * length * LANES + 2 * length * blocks[0].shape[1] * w_own.shape[1],
            length * blocks[0].shape[1] * 4,
            heads * length * length,
        ),
    )(at, *blocks, gm, w_own, table_r, table_c, pick, spread)


def weight_qkv(blocks, attended, own):
    def body(*refs):
        n = len(blocks)
        lefts, rights, out_ref, acc = refs[:n], refs[n : 2 * n], refs[2 * n], refs[2 * n + 1]
        rows = rights[0].shape[0]
        for b in range(n):
            term = dot_tn(lefts[b][:rows, :], rights[b][:, own:])
            if b == 0:
                acc[...] = term
            elif b < n - 1:
                acc[...] += term
            else:
                out_ref[...] = (acc[...] + term).astype(bf16)

    width = blocks[0].shape[1]
    rows = attended[0].shape[0]
    return pl.pallas_call(
        body,
        out_shape=jax.ShapeDtypeStruct((width, 3 * own), bf16),
        in_specs=[VMEM] * (2 * len(blocks)),
        out_specs=VMEM,
        scratch_shapes=[pltpu.VMEM((width, 3 * own), f32)],
        compiler_params=params(48),
        cost_estimate=cost(
            2 * len(blocks) * rows * width * 3 * own, len(blocks) * rows * width * 3
        ),
    )(*blocks, *attended)


def weight_out(attended, cots, own):
    def body(*refs):
        n = len(cots)
        lefts, rights, out_ref = refs[:n], refs[n : 2 * n], refs[2 * n]
        total = dot_tn(lefts[0][:, :own], rights[0][...])
        for b in range(1, n):
            total += dot_tn(lefts[b][:, :own], rights[b][...])
        out_ref[...] = total.astype(bf16)

    rows, width = cots[0].shape
    return pl.pallas_call(
        body,
        out_shape=jax.ShapeDtypeStruct((own, width), bf16),
        in_specs=[VMEM] * (2 * len(cots)),
        out_specs=VMEM,
        compiler_params=params(32),
        cost_estimate=cost(2 * len(cots) * rows * width * own, len(cots) * rows * width * 3),
    )(*attended, *cots)


def finish_kernel(*refs):
    at_ref = refs[0]
    blocks = refs[1:9]
    tok_ref, cot_ref, gain_ref, w_qkv_ref, w_out_ref, result_ref, grad_ref, held, total = refs[9:]
    size = len(blocks)
    own = w_out_ref.shape[0] // size
    t = pl.program_id(0)

    def columns(kind):
        return jnp.concatenate(
            [held[s][:, kind * own : (kind + 1) * own] for s in range(size)], axis=1
        )

    @pl.when(t == 0)
    def _():
        for b, block in enumerate(blocks):
            held[at_ref[b]] = block[...]
        total[...] = dot_nt(columns(1), w_qkv_ref[...])

    for kind in (2, 3):

        @pl.when(t == kind - 1)
        def _(kind=kind):
            total[...] += dot_nt(columns(kind), w_qkv_ref[...])

    @pl.when(t == 3)
    def _():
        wide = tok_ref[...].astype(f32)
        result_ref[...] = (wide + dot_nn(columns(0), w_out_ref[...])).astype(bf16)
        inverse = lax.rsqrt(jnp.mean(wide * wide, axis=-1, keepdims=True) + NORM_EPSILON)
        pre_gain = total[...] * gain_ref[...]
        inner = jnp.mean(pre_gain * wide, axis=-1, keepdims=True)
        grad_x = inverse * pre_gain - (inverse * inverse * inverse) * wide * inner
        grad_ref[...] = (cot_ref[...].astype(f32) + grad_x).astype(bf16)


def finish(at, back, tokens, cotangent, gain, w_qkv, w_out):
    rows, width = tokens.shape
    whole = lambda shape: pl.BlockSpec(shape, lambda t: (0,) * len(shape))
    out = jax.ShapeDtypeStruct((rows, width), bf16)
    return pl.pallas_call(
        finish_kernel,
        grid=(4,),
        out_shape=[out, out],
        in_specs=[SMEM]
        + [whole(back[0].shape)] * len(back)
        + [whole((rows, width))] * 2
        + [
            whole((1, width)),
            pl.BlockSpec((width, width), lambda t: (0, jnp.minimum(t, 2))),
            whole((width, width)),
        ],
        out_specs=[whole((rows, width))] * 2,
        scratch_shapes=[
            pltpu.VMEM((len(back),) + back[0].shape, bf16),
            pltpu.VMEM((rows, width), f32),
        ],
        compiler_params=params(40),
        cost_estimate=cost(8 * rows * width * width, 8 * width * width),
    )(at, *back, tokens, cotangent, gain[None], w_qkv, w_out)


def split3(table):
    first = table.astype(bf16)
    rest = table - first.astype(f32)
    second = rest.astype(bf16)
    third = (rest - second.astype(f32)).astype(bf16)
    return jnp.stack([first, second, third])


def rope_lookup(head_size):
    quarter = head_size // 4
    frequency = ROPE_BASE ** (-jnp.arange(quarter, dtype=f32) / quarter)

    def spread(limit, first):
        angles = jnp.arange(limit, dtype=f32)[:, None] * frequency
        cos, sin = jnp.cos(angles), jnp.sin(angles)
        none = jnp.zeros_like(cos)
        gap = jnp.zeros((limit, HALF - 2 * quarter), f32)
        pair = (lambda x: [x, none, gap]) if first else (lambda x: [none, x, gap])
        return jnp.concatenate(pair(cos) * 2 + pair(-sin) + pair(sin), axis=1)

    return split3(spread(ROW_LIMIT, True)), split3(spread(COL_LIMIT, False))


def gather(value, size):
    mine = [value] + [shift(value, OFFSETS[MIRROR[b]], size) for b in (1, 2, 3)]
    return mine, lambda: [shift(m, (0, 1), size) for m in mine]


def local(tokens, norm_gain, w_qkv, w_out, cotangent, segment, patch_row, patch_col):
    rows, width = tokens.shape
    size = lax.axis_size("seq")
    n_dp = lax.axis_size("dp")
    me = lax.axis_index("seq")
    head_size = width // HEADS
    own = HEADS // size * head_size
    padded = HEADS // size * LANES
    at = [((me // 2 + dz) % (size // 2)) * 2 + ((me % 2) ^ dc) for dz, dc in OFFSETS]
    at = jnp.stack(at).astype(jnp.int32)

    payload = normalise(tokens, norm_gain, segment, patch_row, patch_col)
    mine, others = gather(payload, size)
    blocks = mine + others()
    gm = grad_mixed_blocks(cotangent, w_out, size)
    gm = lax.all_to_all(gm, "seq", split_axis=0, concat_axis=0, tiled=True)

    lane = jnp.arange(padded)
    within = lane % HALF
    source = (lane // LANES) * head_size + (lane % LANES) // HALF * (head_size // 2) + within
    used = within < head_size // 2
    pick = ((source[:, None] == jnp.arange(own)[None, :]) & used[:, None]).astype(bf16)
    expand = ((source[None, :] == jnp.arange(own)[:, None]) & used[None, :]).astype(bf16)
    spread = ((source + me * own)[None, :] == jnp.arange(width)[:, None]) & used[None, :]
    spread = spread.astype(bf16)
    w_own = jnp.concatenate(
        [dot_nn(w_qkv[:, t * width : (t + 1) * width], spread).astype(bf16) for t in range(3)],
        axis=1,
    )
    table_r, table_c = rope_lookup(head_size)

    cot, _ = lax.optimization_barrier((cotangent, mine[3]))
    cot_mine, cot_others = gather(cot, size)

    attended = attend(at, blocks, gm, w_own, table_r, table_c, pick, expand)
    cots = cot_mine + cot_others()

    term_qkv = weight_qkv(blocks, attended, own)
    term_out = weight_out(attended, cots, own)
    chunk = width // n_dp
    terms = jnp.concatenate(
        [term_qkv.reshape(n_dp, chunk, 3 * own), term_out.reshape(n_dp, chunk, own)], axis=2
    )
    tokens_late, terms = lax.optimization_barrier((tokens, terms))
    terms = lax.all_to_all(terms, "dp", split_axis=0, concat_axis=0, tiled=True)

    back = [None] * size
    for b in range(size):
        back[MIRROR[b]] = attended[b] if b == 0 else shift(attended[b], OFFSETS[b], size)
    result, grad_tokens = finish(at, back, tokens_late, cotangent, norm_gain, w_qkv, w_out)

    factor = float(rows * size * n_dp) ** (-0.5)
    terms = jnp.sum(terms.astype(f32), axis=0) * factor
    out_rows = width // (n_dp * size)
    part_qkv = terms[:, : 3 * own].reshape(size, out_rows, 3 * own)
    part_qkv = lax.all_to_all(part_qkv, "seq", split_axis=0, concat_axis=0, tiled=True)
    grad_qkv = part_qkv.reshape(size, out_rows, 3, own).transpose(1, 2, 0, 3)
    grad_qkv = grad_qkv.reshape(out_rows, 3 * width)
    pairs = [(j * size + s, s * n_dp + j) for j in range(n_dp) for s in range(size)]
    grad_out = lax.ppermute(terms[:, 3 * own :].reshape(out_rows, width), ("dp", "seq"), pairs)
    first = (lax.axis_index("dp") * size + me) * out_rows
    w_rows = lax.dynamic_slice(w_qkv, (first, 0), (out_rows, 3 * width)).astype(f32)
    gain_rows = lax.dynamic_slice(norm_gain, (first,), (out_rows,))
    grad_gain = jnp.sum(w_rows * grad_qkv, axis=1) / gain_rows
    return (result, grad_tokens, grad_qkv, grad_out, grad_gain)


def solution(mesh):
    both = P(("dp", "seq"), None)
    flat = P(("dp", "seq"))
    return jax.shard_map(
        local,
        mesh=mesh,
        in_specs=(both, P(), P(), P(), both, flat, flat, flat),
        out_specs=(both, both, both, both, flat),
        check_vma=False,
    )
```

```python
import functools

import jax
import jax.numpy as jnp
from jax import lax
from jax.experimental import pallas as pl
from jax.experimental.pallas import tpu as pltpu
from jax.sharding import PartitionSpec as P

HEADS = 16
NORM_EPSILON = 1e-06
ROPE_BASE = 10000.0
LOG2E = 1.4426950408889634
LANES = 128
HALF = 64
ONE_LANE = 40
BLOCK_Q = 1024
ROW_LIMIT = 256
COL_LIMIT = 128
EXTRA = 16

bf16 = jnp.bfloat16
f32 = jnp.float32

OFFSETS = ((0, 0), (-1, 0), (1, 0), (2, 0), (0, 1), (-1, 1), (1, 1), (2, 1))
MIRROR = (0, 2, 1, 3, 4, 6, 5, 7)
VMEM = pl.BlockSpec(memory_space=pltpu.VMEM)
SMEM = pl.BlockSpec(memory_space=pltpu.SMEM)


def dot_nt(a, b):
    return lax.dot_general(a, b, (((1,), (1,)), ((), ())), preferred_element_type=f32)


def dot_nn(a, b):
    return lax.dot_general(a, b, (((1,), (0,)), ((), ())), preferred_element_type=f32)


def dot_tn(a, b):
    return lax.dot_general(a, b, (((0,), (0,)), ((), ())), preferred_element_type=f32)


def shift(value, offset, size):
    dz, dc = offset
    depth = size // 2
    pairs = [(i, ((i // 2 + dz) % depth) * 2 + ((i % 2) ^ dc)) for i in range(size)]
    return lax.ppermute(value, "seq", pairs)


def params(mib):
    return pltpu.CompilerParams(vmem_limit_bytes=mib * 2**20)


def cost(flops, nbytes, exps=0):
    return pl.CostEstimate(flops=flops, bytes_accessed=nbytes, transcendentals=exps)


def norm_kernel(tok_ref, gain_ref, seg_ref, row_ref, col_ref, out_ref):
    rows = tok_ref.shape[0]
    wide = tok_ref[...].astype(f32)
    inverse = lax.rsqrt(jnp.mean(wide * wide, axis=-1, keepdims=True) + NORM_EPSILON)
    out_ref[:rows, :] = (wide * inverse * gain_ref[...][None, :]).astype(bf16)
    out_ref[rows:, :] = jnp.zeros((EXTRA, out_ref.shape[1]), bf16)
    places = [r[...][None, :].astype(f32) for r in (seg_ref, row_ref, col_ref)]
    places.append(jnp.zeros((EXTRA - 3, rows), f32))
    out_ref[rows:, :rows] = jnp.concatenate(places, axis=0).astype(bf16)


def normalise(tokens, gain, segment, patch_row, patch_col):
    rows, width = tokens.shape
    return pl.pallas_call(
        norm_kernel,
        out_shape=jax.ShapeDtypeStruct((rows + EXTRA, width), bf16),
        in_specs=[VMEM] * 5,
        out_specs=VMEM,
        cost_estimate=cost(8 * rows * width, 4 * rows * width),
    )(tokens, gain, segment, patch_row, patch_col)


def grad_mixed_kernel(cot_ref, w_ref, out_ref):
    size, part, lanes = out_ref.shape
    grad = dot_nt(cot_ref[...], w_ref[...])
    own = w_ref.shape[0] // size
    for s in range(size):
        pieces = [
            grad[i * part : (i + 1) * part, s * own : (s + 1) * own] for i in range(lanes // own)
        ]
        out_ref[s] = jnp.concatenate(pieces, axis=1).astype(bf16)


def grad_mixed_blocks(cotangent, w_out, size):
    rows, width = cotangent.shape
    return pl.pallas_call(
        grad_mixed_kernel,
        out_shape=jax.ShapeDtypeStruct((size, rows // 4, 4 * width // size), bf16),
        in_specs=[VMEM] * 2,
        out_specs=VMEM,
        compiler_params=params(32),
        cost_estimate=cost(2 * rows * width * width, 2 * width * width),
    )(cotangent, w_out)


def attend_kernel(*refs):
    at_ref = refs[0]
    blocks = refs[1:9]
    gm_ref, w_ref, table_r_ref, table_c_ref, pick_ref, spread_ref = refs[9:15]
    outs = refs[15:23]
    term_ref = refs[23]
    q, k, v, g, kt, vt, dk, dv, mixed_pad, dq_pad, cos_t, sin_t, seg_c, seg_r, acc = refs[24:]
    length, padded = q.shape
    heads = padded // LANES
    rows = length // len(blocks)
    own = pick_ref.shape[1]
    scale = 80.0**-0.5
    lane = lax.broadcasted_iota(jnp.int32, (1, padded), 1) % LANES

    def halves(u):
        return jnp.concatenate(
            [pltpu.roll(u[:, h * LANES : (h + 1) * LANES], HALF, 1) for h in range(heads)], axis=1
        )

    for b, block in enumerate(blocks):
        r = slice(b * rows, (b + 1) * rows)
        places = block[rows:, :rows].astype(f32)
        seg_r[:, r] = places[0:1, :]
        columns = places.T
        seg_c[r, :] = columns[:, 0:1]
        rows_at = lax.broadcasted_iota(jnp.int32, (rows, ROW_LIMIT), 1).astype(f32)
        cols_at = lax.broadcasted_iota(jnp.int32, (rows, COL_LIMIT), 1).astype(f32)
        hot_r = (columns[:, 1:2] == rows_at).astype(bf16)
        hot_c = (columns[:, 2:3] == cols_at).astype(bf16)
        cos_b = jnp.zeros((rows, LANES), f32)
        sin_b = jnp.zeros((rows, LANES), f32)
        for piece in range(3):
            found = dot_nn(hot_r, table_r_ref[piece]) + dot_nn(hot_c, table_c_ref[piece])
            cos_b += found[:, :LANES]
            sin_b += found[:, LANES:]
        cos_t[r, :] = cos_b
        sin_t[r, :] = sin_b
        qkv = dot_nn(block[:rows, :], w_ref[...])
        cos2 = jnp.concatenate([cos_b] * heads, axis=1)
        sin2 = jnp.concatenate([sin_b] * heads, axis=1)
        qu = qkv[:, :padded]
        ku = qkv[:, padded : 2 * padded]
        q[r, :] = ((qu * cos2 + halves(qu) * sin2) * (scale * LOG2E)).astype(bf16)
        k[r, :] = (ku * cos2 + halves(ku) * sin2).astype(bf16)
        v[r, :] = jnp.where(lane == ONE_LANE, 1.0, qkv[:, 2 * padded :]).astype(bf16)
        packed = gm_ref[at_ref[b]]
        part = packed.shape[0]
        for i in range(rows // part):
            piece = packed[:, i * own : (i + 1) * own]
            start = b * rows + i * part
            g[start : start + part, :] = dot_nn(piece, spread_ref[...]).astype(bf16)

    for h in range(heads):
        c = slice(h * LANES, (h + 1) * LANES)
        kt[h] = k[:, c].T
        vt[h] = v[:, c].T
    dk[...] = jnp.zeros_like(dk)
    dv[...] = jnp.zeros_like(dv)
    segk = seg_c[...]

    def turn_back(x, start):
        r = pl.ds(start, x.shape[0])
        return x * cos_t[r, :] - pltpu.roll(x, HALF, 1) * sin_t[r, :]

    def step(i, carry):
        start = pl.multiple_of(i * BLOCK_Q, BLOCK_Q)
        r = pl.ds(start, BLOCK_Q)
        same = segk == seg_r[:, r]
        for h in range(heads):
            c = slice(h * LANES, (h + 1) * LANES)
            qb = q[r, c]
            gb = g[r, c]
            st = jnp.where(same, dot_nt(k[:, c], qb), -jnp.inf)
            top = jnp.max(st, axis=0, keepdims=True)
            e = jnp.exp2(st - top).astype(bf16)
            ot = dot_nn(vt[h], e)
            o = ot.T
            inv_col = 1.0 / o[:, ONE_LANE : ONE_LANE + 1]
            inv_row = 1.0 / ot[ONE_LANE : ONE_LANE + 1, :]
            mixed_pad[r, c] = (o * inv_col).astype(bf16)
            centre = jnp.sum(gb.astype(f32).T * ot, axis=0, keepdims=True) * inv_row
            dst = e * (dot_nt(v[:, c], gb) - centre).astype(bf16)
            dqt = dot_nn(kt[h], dst) * (inv_row * scale)
            dq_pad[r, c] = turn_back(dqt.T, start).astype(bf16)
            dk[h] += dot_nn(dst, (qb.astype(f32) * inv_col).astype(bf16))
            dv[h] += dot_nn(e, (gb.astype(f32) * inv_col).astype(bf16))
        return carry

    lax.fori_loop(0, length // BLOCK_Q, step, 0)

    for b in range(len(blocks)):
        start = b * rows
        r = slice(start, start + rows)
        pick = pick_ref[...]
        dk_pad = [turn_back(dk[h, r, :] * (1 / LOG2E), start).astype(bf16) for h in range(heads)]
        dv_pad = [dv[h, r, :].astype(bf16) for h in range(heads)]
        grads = [dq_pad[r, :], jnp.concatenate(dk_pad, axis=1), jnp.concatenate(dv_pad, axis=1)]
        grads = jnp.concatenate([dot_nn(p, pick) for p in grads], axis=1)
        mixed = dot_nn(mixed_pad[r, :], pick)
        outs[b][...] = jnp.concatenate([mixed, grads], axis=1).astype(bf16)
        term = dot_tn(blocks[b][:rows, :], grads.astype(bf16))
        if b == 0:
            acc[...] = term
        elif b < len(blocks) - 1:
            acc[...] += term
        else:
            term_ref[...] = (acc[...] + term).astype(bf16)


def attend(at, blocks, gm, w_own, table_r, table_c, pick, spread):
    rows = blocks[0].shape[0] - EXTRA
    length = rows * len(blocks)
    padded, own = pick.shape
    heads = padded // LANES
    return pl.pallas_call(
        attend_kernel,
        out_shape=[jax.ShapeDtypeStruct((rows, 4 * own), bf16) for _ in blocks]
        + [jax.ShapeDtypeStruct((blocks[0].shape[1], 3 * own), bf16)],
        in_specs=[SMEM] + [VMEM] * (len(blocks) + 6),
        out_specs=[VMEM] * (len(blocks) + 1),
        scratch_shapes=[pltpu.VMEM((length, padded), bf16) for _ in range(4)]
        + [pltpu.VMEM((heads, LANES, length), bf16) for _ in range(2)]
        + [pltpu.VMEM((heads, length, LANES), f32) for _ in range(2)]
        + [pltpu.VMEM((length, padded), bf16) for _ in range(2)]
        + [pltpu.VMEM((length, LANES), f32) for _ in range(2)]
        + [pltpu.VMEM((length, 1), f32), pltpu.VMEM((1, length), f32)]
        + [pltpu.VMEM((blocks[0].shape[1], 3 * own), f32)],
        compiler_params=params(58),
        cost_estimate=cost(
            12 * heads * length * length * LANES + 2 * length * blocks[0].shape[1] * w_own.shape[1],
            length * blocks[0].shape[1] * 4,
            heads * length * length,
        ),
    )(at, *blocks, gm, w_own, table_r, table_c, pick, spread)


def weight_out_kernel(*refs):
    n = (len(refs) - 2) // 2
    lefts, rights, move_ref, out_ref = refs[:n], refs[n : 2 * n], refs[2 * n], refs[2 * n + 1]
    own = out_ref.shape[1]
    total = dot_tn(lefts[0][:, :own], rights[0][...])
    for left, right in zip(lefts[1:], rights[1:]):
        total += dot_tn(left[:, :own], right[...])
    total = total.astype(bf16)
    groups = total.shape[1] // own
    stacked = jnp.concatenate([total[:, i * own : (i + 1) * own] for i in range(groups)], axis=0)
    out_ref[...] = dot_nn(move_ref[...], stacked).astype(bf16)


def weight_out(attended, cots, move, own):
    rows, width = cots[0].shape
    return pl.pallas_call(
        weight_out_kernel,
        out_shape=jax.ShapeDtypeStruct((width, own), bf16),
        in_specs=[VMEM] * (2 * len(cots) + 1),
        out_specs=VMEM,
        compiler_params=params(58),
        cost_estimate=cost(2 * len(cots) * rows * width * own, len(cots) * rows * width * 3),
    )(*attended, *cots, move)


def sum_kernel(factor, own, in_ref, qkv_ref, out_ref):
    total = in_ref[0].astype(f32)
    for i in range(1, in_ref.shape[0]):
        total += in_ref[i].astype(f32)
    total = total * factor
    size, part, columns = qkv_ref.shape
    for s in range(size):
        piece = total[s * part : (s + 1) * part, :]
        qkv_ref[s] = piece[:, :columns]
        out_ref[:, s * own : (s + 1) * own] = piece[:, columns:]


def sum_terms(terms, size, own, factor):
    n_dp, chunk, columns = terms.shape
    part = chunk // size
    return pl.pallas_call(
        functools.partial(sum_kernel, factor, own),
        out_shape=[
            jax.ShapeDtypeStruct((size, part, columns - own), f32),
            jax.ShapeDtypeStruct((part, size * own), f32),
        ],
        in_specs=[VMEM],
        out_specs=[VMEM] * 2,
        compiler_params=params(32),
        cost_estimate=cost(n_dp * chunk * columns, 2 * n_dp * chunk * columns),
    )(terms)


def place_kernel(in_ref, w_ref, gain_ref, qkv_ref, gain_out_ref):
    size, _, columns = in_ref.shape
    own = columns // 3
    for t in range(3):
        for s in range(size):
            start = t * size * own + s * own
            qkv_ref[:, start : start + own] = in_ref[s][:, t * own : (t + 1) * own]
    summed = jnp.sum(qkv_ref[...] * w_ref[...], axis=1, keepdims=True)
    gain_out_ref[...] = summed / gain_ref[...]


def place(parts, w_rows, gain_rows):
    size, rows, columns = parts.shape
    return pl.pallas_call(
        place_kernel,
        out_shape=[
            jax.ShapeDtypeStruct((rows, size * columns), f32),
            jax.ShapeDtypeStruct((rows, 1), f32),
        ],
        in_specs=[VMEM] * 3,
        out_specs=[VMEM] * 2,
        cost_estimate=cost(2 * rows * size * columns, 12 * rows * size * columns),
    )(parts, w_rows, gain_rows)


def finish_kernel(*refs):
    at_ref = refs[0]
    blocks = refs[1:9]
    tok_ref, cot_ref, gain_ref, w_qkv_ref, w_out_ref, result_ref, grad_ref, held, total = refs[9:]
    size = len(blocks)
    own = w_out_ref.shape[0] // size
    t = pl.program_id(0)

    def columns(kind):
        return jnp.concatenate(
            [held[s][:, kind * own : (kind + 1) * own] for s in range(size)], axis=1
        )

    @pl.when(t == 0)
    def _():
        for b, block in enumerate(blocks):
            held[at_ref[b]] = block[...]
        total[...] = dot_nt(columns(1), w_qkv_ref[...])

    for kind in (2, 3):

        @pl.when(t == kind - 1)
        def _(kind=kind):
            total[...] += dot_nt(columns(kind), w_qkv_ref[...])

    @pl.when(t == 3)
    def _():
        wide = tok_ref[...].astype(f32)
        result_ref[...] = (wide + dot_nn(columns(0), w_out_ref[...])).astype(bf16)
        inverse = lax.rsqrt(jnp.mean(wide * wide, axis=-1, keepdims=True) + NORM_EPSILON)
        pre_gain = total[...] * gain_ref[...]
        inner = jnp.mean(pre_gain * wide, axis=-1, keepdims=True)
        grad_x = inverse * pre_gain - (inverse * inverse * inverse) * wide * inner
        grad_ref[...] = (cot_ref[...].astype(f32) + grad_x).astype(bf16)


def finish(at, back, tokens, cotangent, gain, w_qkv, w_out):
    rows, width = tokens.shape
    whole = lambda shape: pl.BlockSpec(shape, lambda t: (0,) * len(shape))
    out = jax.ShapeDtypeStruct((rows, width), bf16)
    return pl.pallas_call(
        finish_kernel,
        grid=(4,),
        out_shape=[out, out],
        in_specs=[SMEM]
        + [whole(back[0].shape)] * len(back)
        + [whole((rows, width))] * 2
        + [
            whole((1, width)),
            pl.BlockSpec((width, width), lambda t: (0, jnp.minimum(t, 2))),
            whole((width, width)),
        ],
        out_specs=[whole((rows, width))] * 2,
        scratch_shapes=[
            pltpu.VMEM((len(back),) + back[0].shape, bf16),
            pltpu.VMEM((rows, width), f32),
        ],
        compiler_params=params(60),
        cost_estimate=cost(8 * rows * width * width, 8 * width * width),
    )(at, *back, tokens, cotangent, gain[None], w_qkv, w_out)


def split3(table):
    first = table.astype(bf16)
    rest = table - first.astype(f32)
    second = rest.astype(bf16)
    third = (rest - second.astype(f32)).astype(bf16)
    return jnp.stack([first, second, third])


def rope_lookup(head_size):
    quarter = head_size // 4
    frequency = ROPE_BASE ** (-jnp.arange(quarter, dtype=f32) / quarter)

    def spread(limit, first):
        angles = jnp.arange(limit, dtype=f32)[:, None] * frequency
        cos, sin = jnp.cos(angles), jnp.sin(angles)
        none = jnp.zeros_like(cos)
        gap = jnp.zeros((limit, HALF - 2 * quarter), f32)
        pair = (lambda x: [x, none, gap]) if first else (lambda x: [none, x, gap])
        return jnp.concatenate(pair(cos) * 2 + pair(-sin) + pair(sin), axis=1)

    return split3(spread(ROW_LIMIT, True)), split3(spread(COL_LIMIT, False))


def gather(value, size):
    mine = [value] + [shift(value, OFFSETS[MIRROR[b]], size) for b in (1, 2, 3)]
    return mine, lambda: [shift(m, (0, 1), size) for m in mine]


def local(tokens, norm_gain, w_qkv, w_out, cotangent, segment, patch_row, patch_col):
    rows, width = tokens.shape
    size = lax.axis_size("seq")
    n_dp = lax.axis_size("dp")
    me = lax.axis_index("seq")
    head_size = width // HEADS
    own = HEADS // size * head_size
    padded = HEADS // size * LANES
    at = [((me // 2 + dz) % (size // 2)) * 2 + ((me % 2) ^ dc) for dz, dc in OFFSETS]
    at = jnp.stack(at).astype(jnp.int32)

    payload = normalise(tokens, norm_gain, segment, patch_row, patch_col)
    mine, others = gather(payload, size)
    blocks = mine + others()
    gm = grad_mixed_blocks(cotangent, w_out, size)
    gm = lax.all_to_all(gm, "seq", split_axis=0, concat_axis=0, tiled=True)

    lane = jnp.arange(padded)
    within = lane % HALF
    source = (lane // LANES) * head_size + (lane % LANES) // HALF * (head_size // 2) + within
    used = within < head_size // 2
    pick = ((source[:, None] == jnp.arange(own)[None, :]) & used[:, None]).astype(bf16)
    expand = ((source[None, :] == jnp.arange(own)[:, None]) & used[None, :]).astype(bf16)
    spread = ((source + me * own)[None, :] == jnp.arange(width)[:, None]) & used[None, :]
    spread = spread.astype(bf16)
    w_own = jnp.concatenate(
        [dot_nn(w_qkv[:, t * width : (t + 1) * width], spread).astype(bf16) for t in range(3)],
        axis=1,
    )
    table_r, table_c = rope_lookup(head_size)

    chunk = width // n_dp
    out_rows = chunk // size
    row = jnp.arange(width)
    moved_from = (row % chunk) // out_rows * own + row // chunk * out_rows + row % out_rows
    move = (moved_from[:, None] == row[None, :]).astype(bf16)
    first = (lax.axis_index("dp") * size + me) * out_rows
    w_rows = lax.dynamic_slice(w_qkv, (first, 0), (out_rows, 3 * width)).astype(f32)
    gain_rows = lax.dynamic_slice(norm_gain, (first,), (out_rows,))[:, None]

    cot, _ = lax.optimization_barrier((cotangent, mine[1:]))
    cot_mine, _ = gather(cot, size)
    *attended, term_qkv = attend(at, blocks, gm, w_own, table_r, table_c, pick, expand)
    cot_mine, attended = lax.optimization_barrier((cot_mine, attended))
    cots = cot_mine + [shift(c, (0, 1), size) for c in cot_mine]

    back = [None] * size
    for b in range(size):
        back[MIRROR[b]] = attended[b] if b == 0 else shift(attended[b], OFFSETS[b], size)

    term_out = weight_out(attended, cots, move, own)
    terms = jnp.concatenate(
        [term_qkv.reshape(n_dp, chunk, 3 * own), term_out.reshape(n_dp, chunk, own)], axis=2
    )
    tokens_late, terms = lax.optimization_barrier((tokens, terms))
    terms = lax.all_to_all(terms, "dp", split_axis=0, concat_axis=0, tiled=True)
    result, grad_tokens = finish(at, back, tokens_late, cotangent, norm_gain, w_qkv, w_out)

    factor = float(rows * size * n_dp) ** (-0.5)
    part_qkv, part_out = sum_terms(terms, size, own, factor)
    part_qkv = lax.all_to_all(part_qkv, "seq", split_axis=0, concat_axis=0, tiled=True)
    pairs = [(j * size + s, s * n_dp + j) for j in range(n_dp) for s in range(size)]
    grad_out = lax.ppermute(part_out, ("dp", "seq"), pairs)
    grad_qkv, grad_gain = place(part_qkv, w_rows, gain_rows)
    return (result, grad_tokens, grad_qkv, grad_out, grad_gain[:, 0])


def solution(mesh):
    both = P(("dp", "seq"), None)
    flat = P(("dp", "seq"))
    return jax.shard_map(
        local,
        mesh=mesh,
        in_specs=(both, P(), P(), P(), both, flat, flat, flat),
        out_specs=(both, both, both, both, flat),
        check_vma=False,
    )
```

```python
import functools

import jax
import jax.numpy as jnp
from jax import lax
from jax.experimental import pallas as pl
from jax.experimental.pallas import tpu as pltpu
from jax.sharding import PartitionSpec as P

HEADS = 16
NORM_EPSILON = 1e-06
ROPE_BASE = 10000.0
LOG2E = 1.4426950408889634
LANES = 128
HALF = 64
ONE_LANE = 40
BLOCK_Q = 1024
ROW_LIMIT = 256
COL_LIMIT = 128
EXTRA = 16

bf16 = jnp.bfloat16
f32 = jnp.float32

OFFSETS = ((0, 0), (-1, 0), (1, 0), (2, 0), (0, 1), (-1, 1), (1, 1), (2, 1))
MIRROR = (0, 2, 1, 3, 4, 6, 5, 7)
VMEM = pl.BlockSpec(memory_space=pltpu.VMEM)
SMEM = pl.BlockSpec(memory_space=pltpu.SMEM)
ANY = pl.BlockSpec(memory_space=pl.ANY)


def dot_nt(a, b):
    return lax.dot_general(a, b, (((1,), (1,)), ((), ())), preferred_element_type=f32)


def dot_nn(a, b):
    return lax.dot_general(a, b, (((1,), (0,)), ((), ())), preferred_element_type=f32)


def dot_tn(a, b):
    return lax.dot_general(a, b, (((0,), (0,)), ((), ())), preferred_element_type=f32)


def shift(value, offset, size):
    dz, dc = offset
    depth = size // 2
    pairs = [(i, ((i // 2 + dz) % depth) * 2 + ((i % 2) ^ dc)) for i in range(size)]
    return lax.ppermute(value, "seq", pairs)


def params(mib):
    return pltpu.CompilerParams(vmem_limit_bytes=mib * 2**20)


def cost(flops, nbytes, exps=0):
    return pl.CostEstimate(flops=flops, bytes_accessed=nbytes, transcendentals=exps)


def norm_kernel(tok_ref, gain_ref, seg_ref, row_ref, col_ref, out_ref):
    rows = tok_ref.shape[0]
    wide = tok_ref[...].astype(f32)
    inverse = lax.rsqrt(jnp.mean(wide * wide, axis=-1, keepdims=True) + NORM_EPSILON)
    out_ref[:rows, :] = (wide * inverse * gain_ref[...][None, :]).astype(bf16)
    out_ref[rows:, :] = jnp.zeros((EXTRA, out_ref.shape[1]), bf16)
    places = [r[...][None, :].astype(f32) for r in (seg_ref, row_ref, col_ref)]
    places.append(jnp.zeros((EXTRA - 3, rows), f32))
    out_ref[rows:, :rows] = jnp.concatenate(places, axis=0).astype(bf16)


def normalise(tokens, gain, segment, patch_row, patch_col):
    rows, width = tokens.shape
    return pl.pallas_call(
        norm_kernel,
        out_shape=jax.ShapeDtypeStruct((rows + EXTRA, width), bf16),
        in_specs=[VMEM] * 5,
        out_specs=VMEM,
        cost_estimate=cost(8 * rows * width, 4 * rows * width),
    )(tokens, gain, segment, patch_row, patch_col)


def grad_mixed_kernel(cot_ref, w_ref, out_ref):
    size, part, lanes = out_ref.shape
    grad = dot_nt(cot_ref[...], w_ref[...])
    own = w_ref.shape[0] // size
    for s in range(size):
        pieces = [
            grad[i * part : (i + 1) * part, s * own : (s + 1) * own] for i in range(lanes // own)
        ]
        out_ref[s] = jnp.concatenate(pieces, axis=1).astype(bf16)


def grad_mixed_blocks(cotangent, w_out, size):
    rows, width = cotangent.shape
    return pl.pallas_call(
        grad_mixed_kernel,
        out_shape=jax.ShapeDtypeStruct((size, rows // 4, 4 * width // size), bf16),
        in_specs=[VMEM] * 2,
        out_specs=VMEM,
        compiler_params=params(32),
        cost_estimate=cost(2 * rows * width * width, 2 * width * width),
    )(cotangent, w_out)


def attend_kernel(*refs):
    at_ref = refs[0]
    blocks = refs[1:9]
    gm_ref, w_ref, table_r_ref, table_c_ref, pick_ref, spread_ref = refs[9:15]
    outs = refs[15:23]
    term_ref, mixed_ref = refs[23:25]
    q, k, v, g, kt, vt, dk, dv, mixed_pad, dq_pad, cos_t, sin_t, seg_c, seg_r, acc = refs[25:]
    length, padded = q.shape
    heads = padded // LANES
    rows = length // len(blocks)
    own = pick_ref.shape[1]
    scale = 80.0**-0.5
    lane = lax.broadcasted_iota(jnp.int32, (1, padded), 1) % LANES

    def halves(u):
        return jnp.concatenate(
            [pltpu.roll(u[:, h * LANES : (h + 1) * LANES], HALF, 1) for h in range(heads)], axis=1
        )

    for b, block in enumerate(blocks):
        r = slice(b * rows, (b + 1) * rows)
        places = block[rows:, :rows].astype(f32)
        seg_r[:, r] = places[0:1, :]
        columns = places.T
        seg_c[r, :] = columns[:, 0:1]
        rows_at = lax.broadcasted_iota(jnp.int32, (rows, ROW_LIMIT), 1).astype(f32)
        cols_at = lax.broadcasted_iota(jnp.int32, (rows, COL_LIMIT), 1).astype(f32)
        hot_r = (columns[:, 1:2] == rows_at).astype(bf16)
        hot_c = (columns[:, 2:3] == cols_at).astype(bf16)
        cos_b = jnp.zeros((rows, LANES), f32)
        sin_b = jnp.zeros((rows, LANES), f32)
        for piece in range(3):
            found = dot_nn(hot_r, table_r_ref[piece]) + dot_nn(hot_c, table_c_ref[piece])
            cos_b += found[:, :LANES]
            sin_b += found[:, LANES:]
        cos_t[r, :] = cos_b
        sin_t[r, :] = sin_b
        qkv = dot_nn(block[:rows, :], w_ref[...])
        cos2 = jnp.concatenate([cos_b] * heads, axis=1)
        sin2 = jnp.concatenate([sin_b] * heads, axis=1)
        qu = qkv[:, :padded]
        ku = qkv[:, padded : 2 * padded]
        q[r, :] = ((qu * cos2 + halves(qu) * sin2) * (scale * LOG2E)).astype(bf16)
        k[r, :] = (ku * cos2 + halves(ku) * sin2).astype(bf16)
        v[r, :] = jnp.where(lane == ONE_LANE, 1.0, qkv[:, 2 * padded :]).astype(bf16)
        packed = gm_ref[at_ref[b]]
        part = packed.shape[0]
        for i in range(rows // part):
            piece = packed[:, i * own : (i + 1) * own]
            start = b * rows + i * part
            g[start : start + part, :] = dot_nn(piece, spread_ref[...]).astype(bf16)

    for h in range(heads):
        c = slice(h * LANES, (h + 1) * LANES)
        kt[h] = k[:, c].T
        vt[h] = v[:, c].T
    dk[...] = jnp.zeros_like(dk)
    dv[...] = jnp.zeros_like(dv)
    segk = seg_c[...]

    def turn_back(x, start):
        r = pl.ds(start, x.shape[0])
        return x * cos_t[r, :] - pltpu.roll(x, HALF, 1) * sin_t[r, :]

    def step(i, carry):
        start = pl.multiple_of(i * BLOCK_Q, BLOCK_Q)
        r = pl.ds(start, BLOCK_Q)
        same = segk == seg_r[:, r]
        for h in range(heads):
            c = slice(h * LANES, (h + 1) * LANES)
            qb = q[r, c]
            gb = g[r, c]
            st = jnp.where(same, dot_nt(k[:, c], qb), -jnp.inf)
            top = jnp.max(st, axis=0, keepdims=True)
            e = jnp.exp2(st - top).astype(bf16)
            ot = dot_nn(vt[h], e)
            o = ot.T
            inv_col = 1.0 / o[:, ONE_LANE : ONE_LANE + 1]
            inv_row = 1.0 / ot[ONE_LANE : ONE_LANE + 1, :]
            mixed_pad[r, c] = (o * inv_col).astype(bf16)
            centre = jnp.sum(gb.astype(f32).T * ot, axis=0, keepdims=True) * inv_row
            dst = e * (dot_nt(v[:, c], gb) - centre).astype(bf16)
            dqt = dot_nn(kt[h], dst) * (inv_row * scale)
            dq_pad[r, c] = turn_back(dqt.T, start).astype(bf16)
            dk[h] += dot_nn(dst, (qb.astype(f32) * inv_col).astype(bf16))
            dv[h] += dot_nn(e, (gb.astype(f32) * inv_col).astype(bf16))
        return carry

    lax.fori_loop(0, length // BLOCK_Q, step, 0)

    for b in range(len(blocks)):
        start = b * rows
        r = slice(start, start + rows)
        pick = pick_ref[...]
        dk_pad = [turn_back(dk[h, r, :] * (1 / LOG2E), start).astype(bf16) for h in range(heads)]
        dv_pad = [dv[h, r, :].astype(bf16) for h in range(heads)]
        grads = [dq_pad[r, :], jnp.concatenate(dk_pad, axis=1), jnp.concatenate(dv_pad, axis=1)]
        grads = jnp.concatenate([dot_nn(p, pick) for p in grads], axis=1)
        mixed = dot_nn(mixed_pad[r, :], pick)
        mixed_ref[r, :] = mixed.astype(bf16)
        outs[b][...] = jnp.concatenate([mixed, grads], axis=1).astype(bf16)
        term = dot_tn(blocks[b][:rows, :], grads.astype(bf16))
        if b == 0:
            acc[...] = term
        elif b < len(blocks) - 1:
            acc[...] += term
        else:
            term_ref[...] = (acc[...] + term).astype(bf16)


def attend(at, blocks, gm, w_own, table_r, table_c, pick, spread):
    rows = blocks[0].shape[0] - EXTRA
    length = rows * len(blocks)
    padded, own = pick.shape
    heads = padded // LANES
    return pl.pallas_call(
        attend_kernel,
        out_shape=[jax.ShapeDtypeStruct((rows, 4 * own), bf16) for _ in blocks]
        + [jax.ShapeDtypeStruct((blocks[0].shape[1], 3 * own), bf16)]
        + [jax.ShapeDtypeStruct((length, own), bf16)],
        in_specs=[SMEM] + [VMEM] * (len(blocks) + 6),
        out_specs=[VMEM] * (len(blocks) + 2),
        scratch_shapes=[pltpu.VMEM((length, padded), bf16) for _ in range(4)]
        + [pltpu.VMEM((heads, LANES, length), bf16) for _ in range(2)]
        + [pltpu.VMEM((heads, length, LANES), f32) for _ in range(2)]
        + [pltpu.VMEM((length, padded), bf16) for _ in range(2)]
        + [pltpu.VMEM((length, LANES), f32) for _ in range(2)]
        + [pltpu.VMEM((length, 1), f32), pltpu.VMEM((1, length), f32)]
        + [pltpu.VMEM((blocks[0].shape[1], 3 * own), f32)],
        compiler_params=params(58),
        cost_estimate=cost(
            12 * heads * length * length * LANES + 2 * length * blocks[0].shape[1] * w_own.shape[1],
            length * blocks[0].shape[1] * 4,
            heads * length * length,
        ),
    )(at, *blocks, gm, w_own, table_r, table_c, pick, spread)


def weight_out_kernel(*refs):
    mixed_hbm, term_hbm, move_hbm = refs[:3]
    n = len(refs) - 9
    cots = refs[3 : 3 + n]
    out_ref, mixed, term, move, held, sems = refs[3 + n :]
    copies = [
        pltpu.make_async_copy(mixed_hbm, mixed, sems.at[0]),
        *[pltpu.make_async_copy(c, held.at[i], sems.at[i + 1]) for i, c in enumerate(cots)],
        pltpu.make_async_copy(move_hbm, move, sems.at[n + 1]),
        pltpu.make_async_copy(term_hbm, term, sems.at[n + 2]),
    ]
    for copy in copies:
        copy.start()
    copies[0].wait()
    n_dp, chunk, _ = out_ref.shape
    rows = held.shape[1]
    own = mixed.shape[1]
    total = None
    for i in range(n):
        copies[i + 1].wait()
        part = dot_tn(mixed[i * rows : (i + 1) * rows, :], held[i])
        total = part if total is None else total + part
    total = total.astype(bf16)
    groups = total.shape[1] // own
    stacked = jnp.concatenate([total[:, i * own : (i + 1) * own] for i in range(groups)], axis=0)
    copies[n + 1].wait()
    moved = dot_nn(move[...], stacked).astype(bf16)
    copies[n + 2].wait()
    for j in range(n_dp):
        r = slice(j * chunk, (j + 1) * chunk)
        out_ref[j] = jnp.concatenate([term[r, :], moved[r, :]], axis=1)


def weight_terms(mixed, term_qkv, move, cots, n_dp):
    rows, width = cots[0].shape
    length, own = mixed.shape
    chunk = width // n_dp
    return pl.pallas_call(
        weight_out_kernel,
        out_shape=jax.ShapeDtypeStruct((n_dp, chunk, 4 * own), bf16),
        in_specs=[ANY] * (len(cots) + 3),
        out_specs=VMEM,
        scratch_shapes=[
            pltpu.VMEM(mixed.shape, bf16),
            pltpu.VMEM(term_qkv.shape, bf16),
            pltpu.VMEM(move.shape, bf16),
            pltpu.VMEM((len(cots), rows, width), bf16),
            pltpu.SemaphoreType.DMA((len(cots) + 3,)),
        ],
        compiler_params=params(60),
        cost_estimate=cost(2 * length * width * own, length * width * 3),
    )(mixed, term_qkv, move, *cots)


def sum_kernel(factor, own, in_ref, qkv_ref, out_ref):
    total = in_ref[0].astype(f32)
    for i in range(1, in_ref.shape[0]):
        total += in_ref[i].astype(f32)
    total = total * factor
    size, part, columns = qkv_ref.shape
    for s in range(size):
        piece = total[s * part : (s + 1) * part, :]
        qkv_ref[s] = piece[:, :columns]
        out_ref[:, s * own : (s + 1) * own] = piece[:, columns:]


def sum_terms(terms, size, own, factor):
    n_dp, chunk, columns = terms.shape
    part = chunk // size
    return pl.pallas_call(
        functools.partial(sum_kernel, factor, own),
        out_shape=[
            jax.ShapeDtypeStruct((size, part, columns - own), f32),
            jax.ShapeDtypeStruct((part, size * own), f32),
        ],
        in_specs=[VMEM],
        out_specs=[VMEM] * 2,
        compiler_params=params(32),
        cost_estimate=cost(n_dp * chunk * columns, 2 * n_dp * chunk * columns),
    )(terms)


def place_kernel(in_ref, w_ref, gain_ref, qkv_ref, gain_out_ref):
    size, _, columns = in_ref.shape
    own = columns // 3
    for t in range(3):
        for s in range(size):
            start = t * size * own + s * own
            qkv_ref[:, start : start + own] = in_ref[s][:, t * own : (t + 1) * own]
    gain_out_ref[...] = jnp.sum(qkv_ref[...] * w_ref[...], axis=1) / gain_ref[...]


def place(parts, w_rows, gain_rows):
    size, rows, columns = parts.shape
    return pl.pallas_call(
        place_kernel,
        out_shape=[
            jax.ShapeDtypeStruct((rows, size * columns), f32),
            jax.ShapeDtypeStruct((rows,), f32),
        ],
        in_specs=[VMEM] * 3,
        out_specs=[VMEM] * 2,
        cost_estimate=cost(2 * rows * size * columns, 12 * rows * size * columns),
    )(parts, w_rows, gain_rows)


def finish_kernel(*refs):
    at_ref = refs[0]
    blocks = refs[1:9]
    tok_ref, cot_ref, gain_ref, w_qkv_ref, w_out_ref, result_ref, grad_ref, held, total = refs[9:]
    size = len(blocks)
    own = w_out_ref.shape[0] // size
    t = pl.program_id(0)

    def columns(kind):
        return jnp.concatenate(
            [held[s][:, kind * own : (kind + 1) * own] for s in range(size)], axis=1
        )

    @pl.when(t == 0)
    def _():
        for b, block in enumerate(blocks):
            held[at_ref[b]] = block[...]
        total[...] = dot_nt(columns(1), w_qkv_ref[...])

    for kind in (2, 3):

        @pl.when(t == kind - 1)
        def _(kind=kind):
            total[...] += dot_nt(columns(kind), w_qkv_ref[...])

    @pl.when(t == 3)
    def _():
        wide = tok_ref[...].astype(f32)
        result_ref[...] = (wide + dot_nn(columns(0), w_out_ref[...])).astype(bf16)
        inverse = lax.rsqrt(jnp.mean(wide * wide, axis=-1, keepdims=True) + NORM_EPSILON)
        pre_gain = total[...] * gain_ref[...][None, :]
        inner = jnp.mean(pre_gain * wide, axis=-1, keepdims=True)
        grad_x = inverse * pre_gain - (inverse * inverse * inverse) * wide * inner
        grad_ref[...] = (cot_ref[...].astype(f32) + grad_x).astype(bf16)


def finish(at, back, tokens, cotangent, gain, w_qkv, w_out):
    rows, width = tokens.shape
    whole = lambda shape: pl.BlockSpec(shape, lambda t: (0,) * len(shape))
    out = jax.ShapeDtypeStruct((rows, width), bf16)
    return pl.pallas_call(
        finish_kernel,
        grid=(4,),
        out_shape=[out, out],
        in_specs=[SMEM]
        + [whole(back[0].shape)] * len(back)
        + [whole((rows, width))] * 2
        + [
            whole((width,)),
            pl.BlockSpec((width, width), lambda t: (0, jnp.minimum(t, 2))),
            whole((width, width)),
        ],
        out_specs=[whole((rows, width))] * 2,
        scratch_shapes=[
            pltpu.VMEM((len(back),) + back[0].shape, bf16),
            pltpu.VMEM((rows, width), f32),
        ],
        compiler_params=params(60),
        cost_estimate=cost(8 * rows * width * width, 8 * width * width),
    )(at, *back, tokens, cotangent, gain, w_qkv, w_out)


def split3(table):
    first = table.astype(bf16)
    rest = table - first.astype(f32)
    second = rest.astype(bf16)
    third = (rest - second.astype(f32)).astype(bf16)
    return jnp.stack([first, second, third])


def rope_lookup(head_size):
    quarter = head_size // 4
    frequency = ROPE_BASE ** (-jnp.arange(quarter, dtype=f32) / quarter)

    def spread(limit, first):
        angles = jnp.arange(limit, dtype=f32)[:, None] * frequency
        cos, sin = jnp.cos(angles), jnp.sin(angles)
        none = jnp.zeros_like(cos)
        gap = jnp.zeros((limit, HALF - 2 * quarter), f32)
        pair = (lambda x: [x, none, gap]) if first else (lambda x: [none, x, gap])
        return jnp.concatenate(pair(cos) * 2 + pair(-sin) + pair(sin), axis=1)

    return split3(spread(ROW_LIMIT, True)), split3(spread(COL_LIMIT, False))


def gather(value, size):
    mine = [value] + [shift(value, OFFSETS[MIRROR[b]], size) for b in (1, 2, 3)]
    return mine, lambda: [shift(m, (0, 1), size) for m in mine]


def local(tokens, norm_gain, w_qkv, w_out, cotangent, segment, patch_row, patch_col):
    rows, width = tokens.shape
    size = lax.axis_size("seq")
    n_dp = lax.axis_size("dp")
    me = lax.axis_index("seq")
    head_size = width // HEADS
    own = HEADS // size * head_size
    padded = HEADS // size * LANES
    at = [((me // 2 + dz) % (size // 2)) * 2 + ((me % 2) ^ dc) for dz, dc in OFFSETS]
    at = jnp.stack(at).astype(jnp.int32)

    payload = normalise(tokens, norm_gain, segment, patch_row, patch_col)
    mine, others = gather(payload, size)
    blocks = mine + others()
    gm = grad_mixed_blocks(cotangent, w_out, size)
    gm = lax.all_to_all(gm, "seq", split_axis=0, concat_axis=0, tiled=True)

    lane = jnp.arange(padded)
    within = lane % HALF
    source = (lane // LANES) * head_size + (lane % LANES) // HALF * (head_size // 2) + within
    used = within < head_size // 2
    pick = ((source[:, None] == jnp.arange(own)[None, :]) & used[:, None]).astype(bf16)
    expand = ((source[None, :] == jnp.arange(own)[:, None]) & used[None, :]).astype(bf16)
    spread = ((source + me * own)[None, :] == jnp.arange(width)[:, None]) & used[None, :]
    spread = spread.astype(bf16)
    w_own = jnp.concatenate(
        [dot_nn(w_qkv[:, t * width : (t + 1) * width], spread).astype(bf16) for t in range(3)],
        axis=1,
    )
    table_r, table_c = rope_lookup(head_size)

    chunk = width // n_dp
    out_rows = chunk // size
    row = jnp.arange(width)
    moved_from = (row % chunk) // out_rows * own + row // chunk * out_rows + row % out_rows
    move = (moved_from[:, None] == row[None, :]).astype(bf16)
    first = (lax.axis_index("dp") * size + me) * out_rows
    w_rows = lax.dynamic_slice(w_qkv, (first, 0), (out_rows, 3 * width)).astype(f32)
    gain_rows = lax.dynamic_slice(norm_gain, (first,), (out_rows,))

    cot, _ = lax.optimization_barrier((cotangent, mine[1:]))
    cot_mine, _ = gather(cot, size)
    *attended, term_qkv, mixed = attend(at, blocks, gm, w_own, table_r, table_c, pick, expand)
    cot_mine, attended = lax.optimization_barrier((cot_mine, attended))
    cots = cot_mine + [shift(c, (0, 1), size) for c in cot_mine]

    back = [None] * size
    for b in range(size):
        back[MIRROR[b]] = attended[b] if b == 0 else shift(attended[b], OFFSETS[b], size)

    terms = weight_terms(mixed, term_qkv, move, cots, n_dp)
    tokens_late, terms = lax.optimization_barrier((tokens, terms))
    terms = lax.all_to_all(terms, "dp", split_axis=0, concat_axis=0, tiled=True)
    result, grad_tokens = finish(at, back, tokens_late, cotangent, norm_gain, w_qkv, w_out)

    factor = float(rows * size * n_dp) ** (-0.5)
    part_qkv, part_out = sum_terms(terms, size, own, factor)
    result, grad_tokens, part_qkv = lax.optimization_barrier((result, grad_tokens, part_qkv))
    part_qkv = lax.all_to_all(part_qkv, "seq", split_axis=0, concat_axis=0, tiled=True)
    pairs = [(j * size + s, s * n_dp + j) for j in range(n_dp) for s in range(size)]
    grad_out = lax.ppermute(part_out, ("dp", "seq"), pairs)
    grad_qkv, grad_gain = place(part_qkv, w_rows, gain_rows)
    return (result, grad_tokens, grad_qkv, grad_out, grad_gain)


def solution(mesh):
    both = P(("dp", "seq"), None)
    flat = P(("dp", "seq"))
    return jax.shard_map(
        local,
        mesh=mesh,
        in_specs=(both, P(), P(), P(), both, flat, flat, flat),
        out_specs=(both, both, both, both, flat),
        check_vma=False,
    )
```

```python
import functools

import jax
import jax.numpy as jnp
from jax import lax
from jax.experimental import pallas as pl
from jax.experimental.pallas import tpu as pltpu
from jax.sharding import PartitionSpec as P

HEADS = 16
NORM_EPSILON = 1e-06
ROPE_BASE = 10000.0
LOG2E = 1.4426950408889634
LANES = 128
HALF = 64
ONE_LANE = 40
BLOCK_Q = 1024
ROW_LIMIT = 256
COL_LIMIT = 128
EXTRA = 16

bf16 = jnp.bfloat16
f32 = jnp.float32

OFFSETS = ((0, 0), (-1, 0), (1, 0), (2, 0), (0, 1), (-1, 1), (1, 1), (2, 1))
MIRROR = (0, 2, 1, 3, 4, 6, 5, 7)
VMEM = pl.BlockSpec(memory_space=pltpu.VMEM)
SMEM = pl.BlockSpec(memory_space=pltpu.SMEM)
ANY = pl.BlockSpec(memory_space=pl.ANY)


def dot_nt(a, b):
    return lax.dot_general(a, b, (((1,), (1,)), ((), ())), preferred_element_type=f32)


def dot_nn(a, b):
    return lax.dot_general(a, b, (((1,), (0,)), ((), ())), preferred_element_type=f32)


def dot_tn(a, b):
    return lax.dot_general(a, b, (((0,), (0,)), ((), ())), preferred_element_type=f32)


def shift(value, offset, size):
    dz, dc = offset
    depth = size // 2
    pairs = [(i, ((i // 2 + dz) % depth) * 2 + ((i % 2) ^ dc)) for i in range(size)]
    return lax.ppermute(value, "seq", pairs)


def params(mib):
    return pltpu.CompilerParams(vmem_limit_bytes=mib * 2**20)


def cost(flops, nbytes, exps=0):
    return pl.CostEstimate(flops=flops, bytes_accessed=nbytes, transcendentals=exps)


def norm_kernel(tok_ref, gain_ref, seg_ref, row_ref, col_ref, out_ref):
    rows = tok_ref.shape[0]
    wide = tok_ref[...].astype(f32)
    inverse = lax.rsqrt(jnp.mean(wide * wide, axis=-1, keepdims=True) + NORM_EPSILON)
    out_ref[:rows, :] = (wide * inverse * gain_ref[...][None, :]).astype(bf16)
    out_ref[rows:, :] = jnp.zeros((EXTRA, out_ref.shape[1]), bf16)
    places = [r[...][None, :].astype(f32) for r in (seg_ref, row_ref, col_ref)]
    places.append(jnp.zeros((EXTRA - 3, rows), f32))
    out_ref[rows:, :rows] = jnp.concatenate(places, axis=0).astype(bf16)


def normalise(tokens, gain, segment, patch_row, patch_col):
    rows, width = tokens.shape
    return pl.pallas_call(
        norm_kernel,
        out_shape=jax.ShapeDtypeStruct((rows + EXTRA, width), bf16),
        in_specs=[VMEM] * 5,
        out_specs=VMEM,
        cost_estimate=cost(8 * rows * width, 4 * rows * width),
    )(tokens, gain, segment, patch_row, patch_col)


def grad_mixed_kernel(cot_ref, w_ref, out_ref):
    size, part, lanes = out_ref.shape
    grad = dot_nt(cot_ref[...], w_ref[...])
    own = w_ref.shape[0] // size
    for s in range(size):
        pieces = [
            grad[i * part : (i + 1) * part, s * own : (s + 1) * own] for i in range(lanes // own)
        ]
        out_ref[s] = jnp.concatenate(pieces, axis=1).astype(bf16)


def grad_mixed_blocks(cotangent, w_out, size):
    rows, width = cotangent.shape
    return pl.pallas_call(
        grad_mixed_kernel,
        out_shape=jax.ShapeDtypeStruct((size, rows // 4, 4 * width // size), bf16),
        in_specs=[VMEM] * 2,
        out_specs=VMEM,
        compiler_params=params(32),
        cost_estimate=cost(2 * rows * width * width, 2 * width * width),
    )(cotangent, w_out)


def attend_kernel(*refs):
    at_ref = refs[0]
    blocks = refs[1:9]
    gm_ref, w_ref, table_r_ref, table_c_ref, pick_ref, spread_ref = refs[9:15]
    outs = refs[15:19]
    term_ref, mixed_ref = refs[19:21]
    q, k, v, g, kt, vt, dk, dv, mixed_pad, dq_pad, cos_t, sin_t, seg_c, seg_r, acc = refs[21:]
    length, padded = q.shape
    heads = padded // LANES
    rows = length // len(blocks)
    own = pick_ref.shape[1]
    scale = 80.0**-0.5
    lane = lax.broadcasted_iota(jnp.int32, (1, padded), 1) % LANES

    def halves(u):
        return jnp.concatenate(
            [pltpu.roll(u[:, h * LANES : (h + 1) * LANES], HALF, 1) for h in range(heads)], axis=1
        )

    for b, block in enumerate(blocks):
        r = slice(b * rows, (b + 1) * rows)
        places = block[rows:, :rows].astype(f32)
        seg_r[:, r] = places[0:1, :]
        columns = places.T
        seg_c[r, :] = columns[:, 0:1]
        rows_at = lax.broadcasted_iota(jnp.int32, (rows, ROW_LIMIT), 1).astype(f32)
        cols_at = lax.broadcasted_iota(jnp.int32, (rows, COL_LIMIT), 1).astype(f32)
        hot_r = (columns[:, 1:2] == rows_at).astype(bf16)
        hot_c = (columns[:, 2:3] == cols_at).astype(bf16)
        cos_b = jnp.zeros((rows, LANES), f32)
        sin_b = jnp.zeros((rows, LANES), f32)
        for piece in range(3):
            found = dot_nn(hot_r, table_r_ref[piece]) + dot_nn(hot_c, table_c_ref[piece])
            cos_b += found[:, :LANES]
            sin_b += found[:, LANES:]
        cos_t[r, :] = cos_b
        sin_t[r, :] = sin_b
        qkv = dot_nn(block[:rows, :], w_ref[...])
        cos2 = jnp.concatenate([cos_b] * heads, axis=1)
        sin2 = jnp.concatenate([sin_b] * heads, axis=1)
        qu = qkv[:, :padded]
        ku = qkv[:, padded : 2 * padded]
        q[r, :] = ((qu * cos2 + halves(qu) * sin2) * (scale * LOG2E)).astype(bf16)
        k[r, :] = (ku * cos2 + halves(ku) * sin2).astype(bf16)
        v[r, :] = jnp.where(lane == ONE_LANE, 1.0, qkv[:, 2 * padded :]).astype(bf16)
        packed = gm_ref[at_ref[b]]
        part = packed.shape[0]
        for i in range(rows // part):
            piece = packed[:, i * own : (i + 1) * own]
            start = b * rows + i * part
            g[start : start + part, :] = dot_nn(piece, spread_ref[...]).astype(bf16)

    for h in range(heads):
        c = slice(h * LANES, (h + 1) * LANES)
        kt[h] = k[:, c].T
        vt[h] = v[:, c].T
    dk[...] = jnp.zeros_like(dk)
    dv[...] = jnp.zeros_like(dv)
    segk = seg_c[...]

    def turn_back(x, start):
        r = pl.ds(start, x.shape[0])
        return x * cos_t[r, :] - pltpu.roll(x, HALF, 1) * sin_t[r, :]

    def step(i, carry):
        start = pl.multiple_of(i * BLOCK_Q, BLOCK_Q)
        r = pl.ds(start, BLOCK_Q)
        same = segk == seg_r[:, r]
        lanes = [slice(h * LANES, (h + 1) * LANES) for h in range(heads)]
        qb = [q[r, c] for c in lanes]
        gb = [g[r, c] for c in lanes]

        def weights(h):
            st = jnp.where(same, dot_nt(k[:, lanes[h]], qb[h]), -jnp.inf)
            return jnp.exp2(st - jnp.max(st, axis=0, keepdims=True)).astype(bf16)

        def forward(h, e):
            ot = dot_nn(vt[h], e)
            o = ot.T
            inv_col = 1.0 / o[:, ONE_LANE : ONE_LANE + 1]
            inv_row = 1.0 / ot[ONE_LANE : ONE_LANE + 1, :]
            mixed_pad[r, lanes[h]] = (o * inv_col).astype(bf16)
            centre = jnp.sum(gb[h].astype(f32).T * ot, axis=0, keepdims=True) * inv_row
            dv[h] += dot_nn(e, (gb[h].astype(f32) * inv_col).astype(bf16))
            return inv_col, inv_row, centre

        def backward(h, e, inv_col, inv_row, centre):
            dst = e * (dot_nt(v[:, lanes[h]], gb[h]) - centre).astype(bf16)
            dqt = dot_nn(kt[h], dst) * (inv_row * scale)
            dq_pad[r, lanes[h]] = turn_back(dqt.T, start).astype(bf16)
            dk[h] += dot_nn(dst, (qb[h].astype(f32) * inv_col).astype(bf16))

        before = None
        for h in range(heads):
            e = weights(h)
            if before is not None:
                backward(*before)
            before = (h, e, *forward(h, e))
        backward(*before)
        return carry

    lax.fori_loop(0, length // BLOCK_Q, step, 0)

    for b in range(len(blocks)):
        start = b * rows
        r = slice(start, start + rows)
        pick = pick_ref[...]
        dk_pad = [turn_back(dk[h, r, :] * (1 / LOG2E), start).astype(bf16) for h in range(heads)]
        dv_pad = [dv[h, r, :].astype(bf16) for h in range(heads)]
        grads = [dq_pad[r, :], jnp.concatenate(dk_pad, axis=1), jnp.concatenate(dv_pad, axis=1)]
        grads = jnp.concatenate([dot_nn(p, pick) for p in grads], axis=1)
        mixed = dot_nn(mixed_pad[r, :], pick)
        mixed_ref[r, :] = mixed.astype(bf16)
        outs[b % 4][b // 4] = jnp.concatenate([mixed, grads], axis=1).astype(bf16)
        term = dot_tn(blocks[b][:rows, :], grads.astype(bf16))
        if b == 0:
            acc[...] = term
        elif b < len(blocks) - 1:
            acc[...] += term
        else:
            term_ref[...] = (acc[...] + term).astype(bf16)


def attend(at, blocks, gm, w_own, table_r, table_c, pick, spread):
    rows = blocks[0].shape[0] - EXTRA
    length = rows * len(blocks)
    padded, own = pick.shape
    heads = padded // LANES
    return pl.pallas_call(
        attend_kernel,
        out_shape=[jax.ShapeDtypeStruct((2, rows, 4 * own), bf16) for _ in range(4)]
        + [jax.ShapeDtypeStruct((blocks[0].shape[1], 3 * own), bf16)]
        + [jax.ShapeDtypeStruct((length, own), bf16)],
        in_specs=[SMEM] + [VMEM] * (len(blocks) + 6),
        out_specs=[VMEM] * 6,
        scratch_shapes=[pltpu.VMEM((length, padded), bf16) for _ in range(4)]
        + [pltpu.VMEM((heads, LANES, length), bf16) for _ in range(2)]
        + [pltpu.VMEM((heads, length, LANES), f32) for _ in range(2)]
        + [pltpu.VMEM((length, padded), bf16) for _ in range(2)]
        + [pltpu.VMEM((length, LANES), f32) for _ in range(2)]
        + [pltpu.VMEM((length, 1), f32), pltpu.VMEM((1, length), f32)]
        + [pltpu.VMEM((blocks[0].shape[1], 3 * own), f32)],
        compiler_params=params(58),
        cost_estimate=cost(
            12 * heads * length * length * LANES + 2 * length * blocks[0].shape[1] * w_own.shape[1],
            length * blocks[0].shape[1] * 4,
            heads * length * length,
        ),
    )(at, *blocks, gm, w_own, table_r, table_c, pick, spread)


def weight_out_kernel(*refs):
    mixed_hbm, term_hbm, move_hbm = refs[:3]
    singles, group = refs[3:8], refs[8]
    out_ref, mixed, term, move, held, sems = refs[9:]
    n = held.shape[0]
    copies = [pltpu.make_async_copy(mixed_hbm, mixed, sems.at[0])]
    for i in range(n):
        source = singles[i] if i < len(singles) else group.at[i - len(singles)]
        copies.append(pltpu.make_async_copy(source, held.at[i], sems.at[i + 1]))
    copies.append(pltpu.make_async_copy(move_hbm, move, sems.at[n + 1]))
    copies.append(pltpu.make_async_copy(term_hbm, term, sems.at[n + 2]))
    for copy in copies:
        copy.start()
    copies[0].wait()
    n_dp, chunk, _ = out_ref.shape
    rows = held.shape[1]
    own = mixed.shape[1]
    total = None
    for i in range(n):
        copies[i + 1].wait()
        part = dot_tn(mixed[i * rows : (i + 1) * rows, :], held[i])
        total = part if total is None else total + part
    total = total.astype(bf16)
    groups = total.shape[1] // own
    copies[n + 1].wait()
    moved = []
    part = move.shape[0] // groups
    for first in range(0, own, part):
        top = total[first : first + part, :]
        stacked = [top[:, i * own : (i + 1) * own] for i in range(groups)]
        moved.append(dot_nn(move[...], jnp.concatenate(stacked, axis=0)).astype(bf16))
    moved = jnp.concatenate(moved, axis=0)
    copies[n + 2].wait()
    for j in range(n_dp):
        r = slice(j * chunk, (j + 1) * chunk)
        out_ref[j] = jnp.concatenate([term[r, :], moved[r, :]], axis=1)


def weight_terms(mixed, term_qkv, move, cots, group, n_dp):
    rows, width = cots[0].shape
    length, own = mixed.shape
    chunk = width // n_dp
    n = len(cots) + group.shape[0]
    return pl.pallas_call(
        weight_out_kernel,
        out_shape=jax.ShapeDtypeStruct((n_dp, chunk, 4 * own), bf16),
        in_specs=[ANY] * (len(cots) + 4),
        out_specs=VMEM,
        scratch_shapes=[
            pltpu.VMEM(mixed.shape, bf16),
            pltpu.VMEM(term_qkv.shape, bf16),
            pltpu.VMEM(move.shape, bf16),
            pltpu.VMEM((n, rows, width), bf16),
            pltpu.SemaphoreType.DMA((n + 3,)),
        ],
        compiler_params=params(60),
        cost_estimate=cost(2 * length * width * own, length * width * 3),
    )(mixed, term_qkv, move, *cots, group)


def sum_kernel(factor, own, in_ref, qkv_ref, out_ref):
    total = in_ref[0].astype(f32)
    for i in range(1, in_ref.shape[0]):
        total += in_ref[i].astype(f32)
    total = total * factor
    size, part, columns = qkv_ref.shape
    for s in range(size):
        piece = total[s * part : (s + 1) * part, :]
        qkv_ref[s] = piece[:, :columns]
        out_ref[:, s * own : (s + 1) * own] = piece[:, columns:]


def sum_terms(terms, size, own, factor):
    n_dp, chunk, columns = terms.shape
    part = chunk // size
    return pl.pallas_call(
        functools.partial(sum_kernel, factor, own),
        out_shape=[
            jax.ShapeDtypeStruct((size, part, columns - own), f32),
            jax.ShapeDtypeStruct((part, size * own), f32),
        ],
        in_specs=[VMEM],
        out_specs=[VMEM] * 2,
        compiler_params=params(32),
        cost_estimate=cost(n_dp * chunk * columns, 2 * n_dp * chunk * columns),
    )(terms)


def place_kernel(in_ref, w_ref, gain_ref, qkv_ref, gain_out_ref):
    size, _, columns = in_ref.shape
    own = columns // 3
    for t in range(3):
        for s in range(size):
            start = t * size * own + s * own
            qkv_ref[:, start : start + own] = in_ref[s][:, t * own : (t + 1) * own]
    gain_out_ref[...] = jnp.sum(qkv_ref[...] * w_ref[...], axis=1) / gain_ref[...]


def place(parts, w_rows, gain_rows):
    size, rows, columns = parts.shape
    return pl.pallas_call(
        place_kernel,
        out_shape=[
            jax.ShapeDtypeStruct((rows, size * columns), f32),
            jax.ShapeDtypeStruct((rows,), f32),
        ],
        in_specs=[VMEM] * 3,
        out_specs=[VMEM] * 2,
        cost_estimate=cost(2 * rows * size * columns, 12 * rows * size * columns),
    )(parts, w_rows, gain_rows)


def finish_kernel(*refs):
    at_ref = refs[0]
    blocks = [ref.at[0] for ref in refs[1:5]] + list(refs[5:9])
    tok_ref, cot_ref, gain_ref, w_qkv_ref, w_out_ref, result_ref, grad_ref, held, total = refs[9:]
    size = len(blocks)
    own = w_out_ref.shape[0] // size
    t = pl.program_id(0)

    def columns(kind):
        return jnp.concatenate(
            [held[s][:, kind * own : (kind + 1) * own] for s in range(size)], axis=1
        )

    @pl.when(t == 0)
    def _():
        for b, block in enumerate(blocks):
            held[at_ref[b]] = block[...]
        total[...] = dot_nt(columns(1), w_qkv_ref[...])

    for kind in (2, 3):

        @pl.when(t == kind - 1)
        def _(kind=kind):
            total[...] += dot_nt(columns(kind), w_qkv_ref[...])

    @pl.when(t == 3)
    def _():
        wide = tok_ref[...].astype(f32)
        result_ref[...] = (wide + dot_nn(columns(0), w_out_ref[...])).astype(bf16)
        inverse = lax.rsqrt(jnp.mean(wide * wide, axis=-1, keepdims=True) + NORM_EPSILON)
        pre_gain = total[...] * gain_ref[...][None, :]
        inner = jnp.mean(pre_gain * wide, axis=-1, keepdims=True)
        grad_x = inverse * pre_gain - (inverse * inverse * inverse) * wide * inner
        grad_ref[...] = (cot_ref[...].astype(f32) + grad_x).astype(bf16)


def finish(at, pairs, cross, tokens, cotangent, gain, w_qkv, w_out):
    rows, width = tokens.shape
    whole = lambda shape: pl.BlockSpec(shape, lambda t: (0,) * len(shape))
    out = jax.ShapeDtypeStruct((rows, width), bf16)
    return pl.pallas_call(
        finish_kernel,
        grid=(4,),
        out_shape=[out, out],
        in_specs=[SMEM]
        + [whole(pairs[0].shape)] * len(pairs)
        + [whole(cross[0].shape)] * len(cross)
        + [whole((rows, width))] * 2
        + [
            whole((width,)),
            pl.BlockSpec((width, width), lambda t: (0, jnp.minimum(t, 2))),
            whole((width, width)),
        ],
        out_specs=[whole((rows, width))] * 2,
        scratch_shapes=[
            pltpu.VMEM((len(pairs) + len(cross),) + cross[0].shape, bf16),
            pltpu.VMEM((rows, width), f32),
        ],
        compiler_params=params(60),
        cost_estimate=cost(32 * rows * width * width, 8 * width * width),
    )(at, *pairs, *cross, tokens, cotangent, gain, w_qkv, w_out)


def split3(table):
    first = table.astype(bf16)
    rest = table - first.astype(f32)
    second = rest.astype(bf16)
    third = (rest - second.astype(f32)).astype(bf16)
    return jnp.stack([first, second, third])


def rope_lookup(head_size):
    quarter = head_size // 4
    frequency = ROPE_BASE ** (-jnp.arange(quarter, dtype=f32) / quarter)

    def spread(limit, first):
        angles = jnp.arange(limit, dtype=f32)[:, None] * frequency
        cos, sin = jnp.cos(angles), jnp.sin(angles)
        none = jnp.zeros_like(cos)
        gap = jnp.zeros((limit, HALF - 2 * quarter), f32)
        pair = (lambda x: [x, none, gap]) if first else (lambda x: [none, x, gap])
        return jnp.concatenate(pair(cos) * 2 + pair(-sin) + pair(sin), axis=1)

    return split3(spread(ROW_LIMIT, True)), split3(spread(COL_LIMIT, False))


def gather(value, size):
    mine = [value] + [shift(value, OFFSETS[MIRROR[b]], size) for b in (1, 2, 3)]
    return mine, lambda: [shift(m, (0, 1), size) for m in mine]


def local(tokens, norm_gain, w_qkv, w_out, cotangent, segment, patch_row, patch_col):
    rows, width = tokens.shape
    size = lax.axis_size("seq")
    n_dp = lax.axis_size("dp")
    me = lax.axis_index("seq")
    head_size = width // HEADS
    own = HEADS // size * head_size
    padded = HEADS // size * LANES
    at = [((me // 2 + dz) % (size // 2)) * 2 + ((me % 2) ^ dc) for dz, dc in OFFSETS]
    at = jnp.stack(at).astype(jnp.int32)

    payload = normalise(tokens, norm_gain, segment, patch_row, patch_col)
    mine, others = gather(payload, size)
    blocks = mine + others()
    gm = grad_mixed_blocks(cotangent, w_out, size)
    gm = lax.all_to_all(gm, "seq", split_axis=0, concat_axis=0, tiled=True)

    lane = jnp.arange(padded)
    within = lane % HALF
    source = (lane // LANES) * head_size + (lane % LANES) // HALF * (head_size // 2) + within
    used = within < head_size // 2
    pick = ((source[:, None] == jnp.arange(own)[None, :]) & used[:, None]).astype(bf16)
    expand = ((source[None, :] == jnp.arange(own)[:, None]) & used[None, :]).astype(bf16)
    spread = ((source + me * own)[None, :] == jnp.arange(width)[:, None]) & used[None, :]
    spread = spread.astype(bf16)
    w_own = jnp.concatenate(
        [dot_nn(w_qkv[:, t * width : (t + 1) * width], spread).astype(bf16) for t in range(3)],
        axis=1,
    )
    table_r, table_c = rope_lookup(head_size)

    chunk = width // n_dp
    out_rows = chunk // size
    half_rows = own // 2
    row = jnp.arange(width // 2)
    moved_from = (row % chunk) // out_rows * half_rows + row // chunk * out_rows + row % out_rows
    move = (moved_from[:, None] == row[None, :]).astype(bf16)
    first = (lax.axis_index("dp") * size + me) * out_rows
    w_rows = lax.dynamic_slice(w_qkv, (first, 0), (out_rows, 3 * width)).astype(f32)
    gain_rows = lax.dynamic_slice(norm_gain, (first,), (out_rows,))

    swapped = shift(cotangent, (0, 1), size)
    cot, _ = lax.optimization_barrier((cotangent, mine[1:]))
    cot_mine, _ = gather(cot, size)
    w_own, move, w_rows, gain_rows, swapped = lax.optimization_barrier(
        (w_own, move, w_rows, gain_rows, swapped)
    )
    *attended, term_qkv, mixed = attend(at, blocks, gm, w_own, table_r, table_c, pick, expand)
    cot_mine, attended = lax.optimization_barrier((cot_mine, attended))
    group = shift(jnp.stack(cot_mine[1:]), (0, 1), size)

    pairs = [attended[0]] + [None] * 3
    for b in (1, 2, 3):
        pairs[MIRROR[b]] = shift(attended[b], OFFSETS[b], size)

    terms = weight_terms(mixed, term_qkv, move, [*cot_mine, swapped], group, n_dp)
    pairs, _ = lax.optimization_barrier((pairs, terms))
    cross = [shift(pair[1], (0, 1), size) for pair in pairs]
    terms = lax.all_to_all(terms, "dp", split_axis=0, concat_axis=0, tiled=True)
    result, grad_tokens = finish(
        at, pairs, cross, tokens, cotangent, norm_gain, w_qkv, w_out
    )

    factor = float(rows * size * n_dp) ** (-0.5)
    part_qkv, part_out = sum_terms(terms, size, own, factor)
    part_qkv = lax.all_to_all(part_qkv, "seq", split_axis=0, concat_axis=0, tiled=True)
    pairs = [(j * size + s, s * n_dp + j) for j in range(n_dp) for s in range(size)]
    grad_out = lax.ppermute(part_out, ("dp", "seq"), pairs)
    grad_qkv, grad_gain = place(part_qkv, w_rows, gain_rows)
    return (result, grad_tokens, grad_qkv, grad_out, grad_gain)


def solution(mesh):
    both = P(("dp", "seq"), None)
    flat = P(("dp", "seq"))
    return jax.shard_map(
        local,
        mesh=mesh,
        in_specs=(both, P(), P(), P(), both, flat, flat, flat),
        out_specs=(both, both, both, both, flat),
        check_vma=False,
    )
```

```python
import functools

import jax
import jax.numpy as jnp
from jax import lax
from jax.experimental import pallas as pl
from jax.experimental.pallas import tpu as pltpu
from jax.sharding import PartitionSpec as P

HEADS = 16
NORM_EPSILON = 1e-06
ROPE_BASE = 10000.0
LOG2E = 1.4426950408889634
LANES = 128
HALF = 64
ONE_LANE = 40
BLOCK_Q = 1024
ROW_LIMIT = 256
COL_LIMIT = 128
EXTRA = 16

bf16 = jnp.bfloat16
f32 = jnp.float32

OFFSETS = ((0, 0), (-1, 0), (1, 0), (2, 0), (0, 1), (-1, 1), (1, 1), (2, 1))
MIRROR = (0, 2, 1, 3, 4, 6, 5, 7)
VMEM = pl.BlockSpec(memory_space=pltpu.VMEM)
SMEM = pl.BlockSpec(memory_space=pltpu.SMEM)
ANY = pl.BlockSpec(memory_space=pl.ANY)


def dot_nt(a, b):
    return lax.dot_general(a, b, (((1,), (1,)), ((), ())), preferred_element_type=f32)


def dot_nn(a, b):
    return lax.dot_general(a, b, (((1,), (0,)), ((), ())), preferred_element_type=f32)


def dot_tn(a, b):
    return lax.dot_general(a, b, (((0,), (0,)), ((), ())), preferred_element_type=f32)


def shift(value, offset, size):
    dz, dc = offset
    depth = size // 2
    pairs = [(i, ((i // 2 + dz) % depth) * 2 + ((i % 2) ^ dc)) for i in range(size)]
    return lax.ppermute(value, "seq", pairs)


def params(mib):
    return pltpu.CompilerParams(vmem_limit_bytes=mib * 2**20)


def cost(flops, nbytes, exps=0):
    return pl.CostEstimate(flops=flops, bytes_accessed=nbytes, transcendentals=exps)


def norm_kernel(tok_ref, gain_ref, seg_ref, row_ref, col_ref, out_ref):
    rows = tok_ref.shape[0]
    wide = tok_ref[...].astype(f32)
    inverse = lax.rsqrt(jnp.mean(wide * wide, axis=-1, keepdims=True) + NORM_EPSILON)
    out_ref[:rows, :] = (wide * inverse * gain_ref[...][None, :]).astype(bf16)
    out_ref[rows:, :] = jnp.zeros((EXTRA, out_ref.shape[1]), bf16)
    places = [r[...][None, :].astype(f32) for r in (seg_ref, row_ref, col_ref)]
    places.append(jnp.zeros((EXTRA - 3, rows), f32))
    out_ref[rows:, :rows] = jnp.concatenate(places, axis=0).astype(bf16)


def normalise(tokens, gain, segment, patch_row, patch_col):
    rows, width = tokens.shape
    return pl.pallas_call(
        norm_kernel,
        out_shape=jax.ShapeDtypeStruct((rows + EXTRA, width), bf16),
        in_specs=[VMEM] * 5,
        out_specs=VMEM,
        cost_estimate=cost(8 * rows * width, 4 * rows * width),
    )(tokens, gain, segment, patch_row, patch_col)


def grad_mixed_kernel(cot_ref, w_ref, out_ref):
    size, part, lanes = out_ref.shape
    grad = dot_nt(cot_ref[...], w_ref[...])
    own = w_ref.shape[0] // size
    for s in range(size):
        pieces = [
            grad[i * part : (i + 1) * part, s * own : (s + 1) * own] for i in range(lanes // own)
        ]
        out_ref[s] = jnp.concatenate(pieces, axis=1).astype(bf16)


def grad_mixed_blocks(cotangent, w_out, size):
    rows, width = cotangent.shape
    return pl.pallas_call(
        grad_mixed_kernel,
        out_shape=jax.ShapeDtypeStruct((size, rows // 4, 4 * width // size), bf16),
        in_specs=[VMEM] * 2,
        out_specs=VMEM,
        compiler_params=params(32),
        cost_estimate=cost(2 * rows * width * width, 2 * width * width),
    )(cotangent, w_out)


def attend_kernel(*refs):
    at_ref = refs[0]
    blocks = refs[1:9]
    gm_ref, w_ref, table_r_ref, table_c_ref, pick_ref, spread_ref = refs[9:15]
    outs = refs[15:19]
    term_ref, mixed_ref = refs[19:21]
    q, k, v, g, kt, vt, dk, dv, mixed_pad, dq_pad, cos_t, sin_t, seg_c, seg_r, acc = refs[21:]
    length, padded = q.shape
    heads = padded // LANES
    rows = length // len(blocks)
    own = pick_ref.shape[1]
    scale = 80.0**-0.5
    lane = lax.broadcasted_iota(jnp.int32, (1, padded), 1) % LANES

    def halves(u):
        return jnp.concatenate(
            [pltpu.roll(u[:, h * LANES : (h + 1) * LANES], HALF, 1) for h in range(heads)], axis=1
        )

    for b, block in enumerate(blocks):
        r = slice(b * rows, (b + 1) * rows)
        places = block[rows:, :rows].astype(f32)
        seg_r[:, r] = places[0:1, :]
        columns = places.T
        seg_c[r, :] = columns[:, 0:1]
        rows_at = lax.broadcasted_iota(jnp.int32, (rows, ROW_LIMIT), 1).astype(f32)
        cols_at = lax.broadcasted_iota(jnp.int32, (rows, COL_LIMIT), 1).astype(f32)
        hot_r = (columns[:, 1:2] == rows_at).astype(bf16)
        hot_c = (columns[:, 2:3] == cols_at).astype(bf16)
        cos_b = jnp.zeros((rows, LANES), f32)
        sin_b = jnp.zeros((rows, LANES), f32)
        for piece in range(3):
            found = dot_nn(hot_r, table_r_ref[piece]) + dot_nn(hot_c, table_c_ref[piece])
            cos_b += found[:, :LANES]
            sin_b += found[:, LANES:]
        cos_t[r, :] = cos_b
        sin_t[r, :] = sin_b
        qkv = dot_nn(block[:rows, :], w_ref[...])
        cos2 = jnp.concatenate([cos_b] * heads, axis=1)
        sin2 = jnp.concatenate([sin_b] * heads, axis=1)
        qu = qkv[:, :padded]
        ku = qkv[:, padded : 2 * padded]
        q[r, :] = ((qu * cos2 + halves(qu) * sin2) * (scale * LOG2E)).astype(bf16)
        k[r, :] = (ku * cos2 + halves(ku) * sin2).astype(bf16)
        v[r, :] = jnp.where(lane == ONE_LANE, 1.0, qkv[:, 2 * padded :]).astype(bf16)
        packed = gm_ref[at_ref[b]]
        part = packed.shape[0]
        for i in range(rows // part):
            piece = packed[:, i * own : (i + 1) * own]
            start = b * rows + i * part
            g[start : start + part, :] = dot_nn(piece, spread_ref[...]).astype(bf16)

    for h in range(heads):
        c = slice(h * LANES, (h + 1) * LANES)
        kt[h] = k[:, c].T
        vt[h] = v[:, c].T
    dk[...] = jnp.zeros_like(dk)
    dv[...] = jnp.zeros_like(dv)
    segk = seg_c[...]

    def turn_back(x, start):
        r = pl.ds(start, x.shape[0])
        return x * cos_t[r, :] - pltpu.roll(x, HALF, 1) * sin_t[r, :]

    def step(i, carry):
        start = pl.multiple_of(i * BLOCK_Q, BLOCK_Q)
        r = pl.ds(start, BLOCK_Q)
        same = segk == seg_r[:, r]
        lanes = [slice(h * LANES, (h + 1) * LANES) for h in range(heads)]
        qb = [q[r, c] for c in lanes]
        gb = [g[r, c] for c in lanes]

        def weights(h):
            st = jnp.where(same, dot_nt(k[:, lanes[h]], qb[h]), -jnp.inf)
            return jnp.exp2(st - jnp.max(st, axis=0, keepdims=True)).astype(bf16)

        def forward(h, e):
            ot = dot_nn(vt[h], e)
            o = ot.T
            inv_col = 1.0 / o[:, ONE_LANE : ONE_LANE + 1]
            inv_row = 1.0 / ot[ONE_LANE : ONE_LANE + 1, :]
            mixed_pad[r, lanes[h]] = (o * inv_col).astype(bf16)
            centre = jnp.sum(gb[h].astype(f32).T * ot, axis=0, keepdims=True) * inv_row
            dv[h] += dot_nn(e, (gb[h].astype(f32) * inv_col).astype(bf16))
            return inv_col, inv_row, centre

        def backward(h, e, inv_col, inv_row, centre):
            dst = e * (dot_nt(v[:, lanes[h]], gb[h]) - centre).astype(bf16)
            dqt = dot_nn(kt[h], dst) * (inv_row * scale)
            dq_pad[r, lanes[h]] = turn_back(dqt.T, start).astype(bf16)
            dk[h] += dot_nn(dst, (qb[h].astype(f32) * inv_col).astype(bf16))

        before = None
        for h in range(heads):
            e = weights(h)
            if before is not None:
                backward(*before)
            before = (h, e, *forward(h, e))
        backward(*before)
        return carry

    lax.fori_loop(0, length // BLOCK_Q, step, 0)

    for b in range(len(blocks)):
        start = b * rows
        r = slice(start, start + rows)
        pick = pick_ref[...]
        dk_pad = [turn_back(dk[h, r, :] * (1 / LOG2E), start).astype(bf16) for h in range(heads)]
        dv_pad = [dv[h, r, :].astype(bf16) for h in range(heads)]
        grads = [dq_pad[r, :], jnp.concatenate(dk_pad, axis=1), jnp.concatenate(dv_pad, axis=1)]
        grads = jnp.concatenate([dot_nn(p, pick) for p in grads], axis=1)
        mixed = dot_nn(mixed_pad[r, :], pick)
        mixed_ref[r, :] = mixed.astype(bf16)
        outs[b % 4][b // 4] = jnp.concatenate([mixed, grads], axis=1).astype(bf16)
        term = dot_tn(blocks[b][:rows, :], grads.astype(bf16))
        if b == 0:
            acc[...] = term
        elif b < len(blocks) - 1:
            acc[...] += term
        else:
            term_ref[...] = (acc[...] + term).astype(bf16)


def attend(at, blocks, gm, w_own, table_r, table_c, pick, spread):
    rows = blocks[0].shape[0] - EXTRA
    length = rows * len(blocks)
    padded, own = pick.shape
    heads = padded // LANES
    return pl.pallas_call(
        attend_kernel,
        out_shape=[jax.ShapeDtypeStruct((2, rows, 4 * own), bf16) for _ in range(4)]
        + [jax.ShapeDtypeStruct((blocks[0].shape[1], 3 * own), bf16)]
        + [jax.ShapeDtypeStruct((length, own), bf16)],
        in_specs=[SMEM] + [VMEM] * (len(blocks) + 6),
        out_specs=[VMEM] * 6,
        scratch_shapes=[pltpu.VMEM((length, padded), bf16) for _ in range(4)]
        + [pltpu.VMEM((heads, LANES, length), bf16) for _ in range(2)]
        + [pltpu.VMEM((heads, length, LANES), f32) for _ in range(2)]
        + [pltpu.VMEM((length, padded), bf16) for _ in range(2)]
        + [pltpu.VMEM((length, LANES), f32) for _ in range(2)]
        + [pltpu.VMEM((length, 1), f32), pltpu.VMEM((1, length), f32)]
        + [pltpu.VMEM((blocks[0].shape[1], 3 * own), f32)],
        compiler_params=params(58),
        cost_estimate=cost(
            12 * heads * length * length * LANES + 2 * length * blocks[0].shape[1] * w_own.shape[1],
            length * blocks[0].shape[1] * 4,
            heads * length * length,
        ),
    )(at, *blocks, gm, w_own, table_r, table_c, pick, spread)


def weight_out_kernel(
    mixed_hbm, term_hbm, move_hbm, c0, c1, c2, c3, c7, out_ref, mixed, term, move, held, sems
):
    n = held.shape[0]
    copies = [pltpu.make_async_copy(mixed_hbm, mixed, sems.at[0])]
    for i in range(n):
        source = (c3, c7)[i // 4] if i % 4 == 3 else (c0, c1, c2)[i % 4].at[i // 4]
        copies.append(pltpu.make_async_copy(source, held.at[i], sems.at[i + 1]))
    copies.append(pltpu.make_async_copy(move_hbm, move, sems.at[n + 1]))
    copies.append(pltpu.make_async_copy(term_hbm, term, sems.at[n + 2]))
    for copy in copies:
        copy.start()
    copies[0].wait()
    n_dp, chunk, _ = out_ref.shape
    rows = held.shape[1]
    own = mixed.shape[1]
    total = None
    for i in range(n):
        copies[i + 1].wait()
        part = dot_tn(mixed[i * rows : (i + 1) * rows, :], held[i])
        total = part if total is None else total + part
    total = total.astype(bf16)
    groups = total.shape[1] // own
    copies[n + 1].wait()
    moved = []
    part = move.shape[0] // groups
    for first in range(0, own, part):
        top = total[first : first + part, :]
        stacked = [top[:, i * own : (i + 1) * own] for i in range(groups)]
        moved.append(dot_nn(move[...], jnp.concatenate(stacked, axis=0)).astype(bf16))
    moved = jnp.concatenate(moved, axis=0)
    copies[n + 2].wait()
    for j in range(n_dp):
        r = slice(j * chunk, (j + 1) * chunk)
        out_ref[j] = jnp.concatenate([term[r, :], moved[r, :]], axis=1)


def weight_terms(mixed, term_qkv, move, cots, n_dp):
    _, rows, width = cots[0].shape
    length, own = mixed.shape
    chunk = width // n_dp
    n = length // rows
    return pl.pallas_call(
        weight_out_kernel,
        out_shape=jax.ShapeDtypeStruct((n_dp, chunk, 4 * own), bf16),
        in_specs=[ANY] * (len(cots) + 3),
        out_specs=VMEM,
        scratch_shapes=[
            pltpu.VMEM(mixed.shape, bf16),
            pltpu.VMEM(term_qkv.shape, bf16),
            pltpu.VMEM(move.shape, bf16),
            pltpu.VMEM((n, rows, width), bf16),
            pltpu.SemaphoreType.DMA((n + 3,)),
        ],
        compiler_params=params(60),
        cost_estimate=cost(2 * length * width * own, length * width * 3),
    )(mixed, term_qkv, move, *cots)


def sum_kernel(factor, own, in_ref, qkv_ref, out_ref):
    total = in_ref[0].astype(f32)
    for i in range(1, in_ref.shape[0]):
        total += in_ref[i].astype(f32)
    total = total * factor
    size, part, columns = qkv_ref.shape
    for s in range(size):
        piece = total[s * part : (s + 1) * part, :]
        qkv_ref[s] = piece[:, :columns]
        out_ref[:, s * own : (s + 1) * own] = piece[:, columns:]


def sum_terms(terms, size, own, factor):
    n_dp, chunk, columns = terms.shape
    part = chunk // size
    return pl.pallas_call(
        functools.partial(sum_kernel, factor, own),
        out_shape=[
            jax.ShapeDtypeStruct((size, part, columns - own), f32),
            jax.ShapeDtypeStruct((part, size * own), f32),
        ],
        in_specs=[VMEM],
        out_specs=[VMEM] * 2,
        compiler_params=params(32),
        cost_estimate=cost(n_dp * chunk * columns, 2 * n_dp * chunk * columns),
    )(terms)


def place_kernel(in_ref, w_ref, gain_ref, qkv_ref, gain_out_ref):
    size, _, columns = in_ref.shape
    own = columns // 3
    for t in range(3):
        for s in range(size):
            start = t * size * own + s * own
            qkv_ref[:, start : start + own] = in_ref[s][:, t * own : (t + 1) * own]
    gain_out_ref[...] = jnp.sum(qkv_ref[...] * w_ref[...], axis=1) / gain_ref[...]


def place(parts, w_rows, gain_rows):
    size, rows, columns = parts.shape
    return pl.pallas_call(
        place_kernel,
        out_shape=[
            jax.ShapeDtypeStruct((rows, size * columns), f32),
            jax.ShapeDtypeStruct((rows,), f32),
        ],
        in_specs=[VMEM] * 3,
        out_specs=[VMEM] * 2,
        cost_estimate=cost(2 * rows * size * columns, 12 * rows * size * columns),
    )(parts, w_rows, gain_rows)


def finish_kernel(
    from_ref, p0, p1, p2, p3, c0, c1, c2, c3, w_qkv_hbm, w_out_hbm, tok_ref, cot_ref, gain_ref,
    result_ref, grad_ref, held, weights, sides, sems,
):
    size = held.shape[0]
    width = tok_ref.shape[1]
    own = width // size
    blocks = [p0.at[0], p1.at[0], p2.at[0], p3.at[0], c0, c1, c2, c3]
    sources = [w_out_hbm] + [w_qkv_hbm.at[:, pl.ds(t * width, width)] for t in range(3)]
    copies = [pltpu.make_async_copy(b, held.at[i], sems.at[i]) for i, b in enumerate(blocks)]
    loads = [
        pltpu.make_async_copy(w, weights.at[i], sems.at[size + i]) for i, w in enumerate(sources)
    ]
    for copy in copies + loads:
        copy.start()
    for copy in copies:
        copy.wait()
    for kind in range(4):
        parts = [held[from_ref[s], :, kind * own : (kind + 1) * own] for s in range(size)]
        sides[kind] = jnp.concatenate(parts, axis=1)
    wide = tok_ref[...].astype(f32)
    loads[0].wait()
    result_ref[...] = (wide + dot_nn(sides[0], weights[0])).astype(bf16)
    loads[1].wait()
    total = dot_nt(sides[1], weights[1])
    for kind in (2, 3):
        loads[kind].wait()
        total += dot_nt(sides[kind], weights[kind])
    inverse = lax.rsqrt(jnp.mean(wide * wide, axis=-1, keepdims=True) + NORM_EPSILON)
    pre_gain = total * gain_ref[...][None, :]
    inner = jnp.mean(pre_gain * wide, axis=-1, keepdims=True)
    grad_x = inverse * pre_gain - (inverse * inverse * inverse) * wide * inner
    grad_ref[...] = (cot_ref[...].astype(f32) + grad_x).astype(bf16)


def finish(source, pairs, cross, tokens, cotangent, gain, w_qkv, w_out):
    rows, width = tokens.shape
    n = len(pairs) + len(cross)
    out = jax.ShapeDtypeStruct((rows, width), bf16)
    return pl.pallas_call(
        finish_kernel,
        out_shape=[out, out],
        in_specs=[SMEM] + [ANY] * (n + 2) + [VMEM] * 3,
        out_specs=[VMEM] * 2,
        scratch_shapes=[
            pltpu.VMEM((n,) + cross[0].shape, bf16),
            pltpu.VMEM((4, width, width), bf16),
            pltpu.VMEM((4, rows, width), bf16),
            pltpu.SemaphoreType.DMA((n + 4,)),
        ],
        compiler_params=params(60),
        cost_estimate=cost(32 * rows * width * width, 8 * width * width),
    )(source, *pairs, *cross, w_qkv, w_out, tokens, cotangent, gain)


def split3(table):
    first = table.astype(bf16)
    rest = table - first.astype(f32)
    second = rest.astype(bf16)
    third = (rest - second.astype(f32)).astype(bf16)
    return jnp.stack([first, second, third])


def rope_lookup(head_size):
    quarter = head_size // 4
    frequency = ROPE_BASE ** (-jnp.arange(quarter, dtype=f32) / quarter)

    def spread(limit, first):
        angles = jnp.arange(limit, dtype=f32)[:, None] * frequency
        cos, sin = jnp.cos(angles), jnp.sin(angles)
        none = jnp.zeros_like(cos)
        gap = jnp.zeros((limit, HALF - 2 * quarter), f32)
        pair = (lambda x: [x, none, gap]) if first else (lambda x: [none, x, gap])
        return jnp.concatenate(pair(cos) * 2 + pair(-sin) + pair(sin), axis=1)

    return split3(spread(ROW_LIMIT, True)), split3(spread(COL_LIMIT, False))


def gather(value, size):
    return [value] + [shift(value, OFFSETS[MIRROR[b]], size) for b in (1, 2, 3)]


def local(tokens, norm_gain, w_qkv, w_out, cotangent, segment, patch_row, patch_col):
    rows, width = tokens.shape
    size = lax.axis_size("seq")
    n_dp = lax.axis_size("dp")
    me = lax.axis_index("seq")
    head_size = width // HEADS
    own = HEADS // size * head_size
    padded = HEADS // size * LANES
    at = [((me // 2 + dz) % (size // 2)) * 2 + ((me % 2) ^ dc) for dz, dc in OFFSETS]
    at = jnp.stack(at).astype(jnp.int32)
    every = jnp.arange(size)
    steps = (every // 2 - me // 2) % (size // 2)
    source_of = jnp.where(steps == 0, 0, jnp.where(steps == size // 2 - 1, 1, steps + 1))
    source_of = (source_of + size // 2 * ((every % 2) ^ (me % 2))).astype(jnp.int32)

    payload = normalise(tokens, norm_gain, segment, patch_row, patch_col)
    mine = gather(payload, size)
    own_swap = shift(payload, (0, 1), size)
    cot_pair = jnp.stack([cotangent, shift(cotangent, (0, 1), size)])
    blocks = mine + [own_swap] + [shift(m, (0, 1), size) for m in mine[1:]]
    gm = grad_mixed_blocks(cotangent, w_out, size)
    gm = lax.all_to_all(gm, "seq", split_axis=0, concat_axis=0, tiled=True)

    lane = jnp.arange(padded)
    within = lane % HALF
    source = (lane // LANES) * head_size + (lane % LANES) // HALF * (head_size // 2) + within
    used = within < head_size // 2
    pick = ((source[:, None] == jnp.arange(own)[None, :]) & used[:, None]).astype(bf16)
    expand = ((source[None, :] == jnp.arange(own)[:, None]) & used[None, :]).astype(bf16)
    spread = ((source + me * own)[None, :] == jnp.arange(width)[:, None]) & used[None, :]
    spread = spread.astype(bf16)
    w_own = jnp.concatenate(
        [dot_nn(w_qkv[:, t * width : (t + 1) * width], spread).astype(bf16) for t in range(3)],
        axis=1,
    )
    table_r, table_c = rope_lookup(head_size)

    chunk = width // n_dp
    out_rows = chunk // size
    half_rows = own // 2
    row = jnp.arange(width // 2)
    moved_from = (row % chunk) // out_rows * half_rows + row // chunk * out_rows + row % out_rows
    move = (moved_from[:, None] == row[None, :]).astype(bf16)
    cot_pair, cot, _ = lax.optimization_barrier((cot_pair, cotangent, (mine[1:], own_swap)))
    cots = [cot_pair] + [shift(cot_pair, OFFSETS[MIRROR[b]], size) for b in (1, 2)]
    cots.append(shift(cot, OFFSETS[MIRROR[3]], size))
    w_own, move = lax.optimization_barrier((w_own, move))
    *attended, term_qkv, mixed = attend(at, blocks, gm, w_own, table_r, table_c, pick, expand)
    cots, attended = lax.optimization_barrier((cots, attended))
    cots.append(shift(cots[3], (0, 1), size))

    pairs = [attended[0]] + [None] * 3
    for b in (1, 2, 3):
        pairs[MIRROR[b]] = shift(attended[b], OFFSETS[b], size)

    terms = weight_terms(mixed, term_qkv, move, cots, n_dp)
    first = (lax.axis_index("dp") * size + me) * out_rows
    first, _ = lax.optimization_barrier((first, terms))
    pairs, _ = lax.optimization_barrier((pairs, terms))
    w_rows = lax.dynamic_slice(w_qkv, (first, 0), (out_rows, 3 * width)).astype(f32)
    gain_rows = lax.dynamic_slice(norm_gain, (first,), (out_rows,))
    cross = [shift(pair[1], (0, 1), size) for pair in pairs]
    terms = lax.all_to_all(terms, "dp", split_axis=0, concat_axis=0, tiled=True)
    result, grad_tokens = finish(
        source_of, pairs, cross, tokens, cotangent, norm_gain, w_qkv, w_out
    )

    factor = float(rows * size * n_dp) ** (-0.5)
    part_qkv, part_out = sum_terms(terms, size, own, factor)
    part_qkv = lax.all_to_all(part_qkv, "seq", split_axis=0, concat_axis=0, tiled=True)
    pairs = [(j * size + s, s * n_dp + j) for j in range(n_dp) for s in range(size)]
    grad_out = lax.ppermute(part_out, ("dp", "seq"), pairs)
    grad_qkv, grad_gain = place(part_qkv, w_rows, gain_rows)
    return (result, grad_tokens, grad_qkv, grad_out, grad_gain)


def solution(mesh):
    both = P(("dp", "seq"), None)
    flat = P(("dp", "seq"))
    return jax.shard_map(
        local,
        mesh=mesh,
        in_specs=(both, P(), P(), P(), both, flat, flat, flat),
        out_specs=(both, both, both, both, flat),
        check_vma=False,
    )
```

```python
import functools

import jax
import jax.numpy as jnp
from jax import lax
from jax.experimental import pallas as pl
from jax.experimental.pallas import tpu as pltpu
from jax.sharding import PartitionSpec as P

HEADS = 16
NORM_EPSILON = 1e-06
ROPE_BASE = 10000.0
LOG2E = 1.4426950408889634
LANES = 128
HALF = 64
ONE_LANE = 40
BLOCK_Q = 1024
ROW_LIMIT = 256
COL_LIMIT = 128
EXTRA = 16

bf16 = jnp.bfloat16
f32 = jnp.float32

OFFSETS = ((0, 0), (-1, 0), (1, 0), (2, 0), (0, 1), (-1, 1), (1, 1), (2, 1))
MIRROR = (0, 2, 1, 3, 4, 6, 5, 7)
VMEM = pl.BlockSpec(memory_space=pltpu.VMEM)
SMEM = pl.BlockSpec(memory_space=pltpu.SMEM)
ANY = pl.BlockSpec(memory_space=pl.ANY)


def dot_nt(a, b):
    return lax.dot_general(a, b, (((1,), (1,)), ((), ())), preferred_element_type=f32)


def dot_nn(a, b):
    return lax.dot_general(a, b, (((1,), (0,)), ((), ())), preferred_element_type=f32)


def dot_tn(a, b):
    return lax.dot_general(a, b, (((0,), (0,)), ((), ())), preferred_element_type=f32)


def shift(value, offset, size):
    dz, dc = offset
    depth = size // 2
    pairs = [(i, ((i // 2 + dz) % depth) * 2 + ((i % 2) ^ dc)) for i in range(size)]
    return lax.ppermute(value, "seq", pairs)


def params(mib):
    return pltpu.CompilerParams(vmem_limit_bytes=mib * 2**20)


def cost(flops, nbytes, exps=0):
    return pl.CostEstimate(flops=flops, bytes_accessed=nbytes, transcendentals=exps)


def norm_kernel(tok_ref, gain_ref, seg_ref, row_ref, col_ref, out_ref):
    rows = tok_ref.shape[0]
    wide = tok_ref[...].astype(f32)
    inverse = lax.rsqrt(jnp.mean(wide * wide, axis=-1, keepdims=True) + NORM_EPSILON)
    out_ref[:rows, :] = (wide * inverse * gain_ref[...][None, :]).astype(bf16)
    out_ref[rows:, :] = jnp.zeros((EXTRA, out_ref.shape[1]), bf16)
    places = [r[...][None, :].astype(f32) for r in (seg_ref, row_ref, col_ref)]
    places.append(jnp.zeros((EXTRA - 3, rows), f32))
    out_ref[rows:, :rows] = jnp.concatenate(places, axis=0).astype(bf16)


def normalise(tokens, gain, segment, patch_row, patch_col):
    rows, width = tokens.shape
    return pl.pallas_call(
        norm_kernel,
        out_shape=jax.ShapeDtypeStruct((rows + EXTRA, width), bf16),
        in_specs=[VMEM] * 5,
        out_specs=VMEM,
        cost_estimate=cost(8 * rows * width, 4 * rows * width),
    )(tokens, gain, segment, patch_row, patch_col)


def grad_mixed_kernel(cot_ref, w_ref, out_ref):
    size, part, lanes = out_ref.shape
    grad = dot_nt(cot_ref[...], w_ref[...])
    own = w_ref.shape[0] // size
    for s in range(size):
        pieces = [
            grad[i * part : (i + 1) * part, s * own : (s + 1) * own] for i in range(lanes // own)
        ]
        out_ref[s] = jnp.concatenate(pieces, axis=1).astype(bf16)


def grad_mixed_blocks(cotangent, w_out, size):
    rows, width = cotangent.shape
    return pl.pallas_call(
        grad_mixed_kernel,
        out_shape=jax.ShapeDtypeStruct((size, rows // 4, 4 * width // size), bf16),
        in_specs=[VMEM] * 2,
        out_specs=VMEM,
        compiler_params=params(32),
        cost_estimate=cost(2 * rows * width * width, 2 * width * width),
    )(cotangent, w_out)


def attend_kernel(*refs):
    at_ref = refs[0]
    blocks = refs[1:9]
    gm_ref, w_ref, table_r_ref, table_c_ref, pick_ref, spread_ref = refs[9:15]
    outs = refs[15:19]
    term_ref, mixed_ref = refs[19:21]
    q, k, v, g, kt, vt, dk, dv, mixed_pad, dq_pad, cos_t, sin_t, seg_c, seg_r, grads_all = refs[21:]
    length, padded = q.shape
    heads = padded // LANES
    rows = length // len(blocks)
    own = pick_ref.shape[1]
    scale = 80.0**-0.5
    lane = lax.broadcasted_iota(jnp.int32, (1, padded), 1) % LANES

    def halves(u):
        return jnp.concatenate(
            [pltpu.roll(u[:, h * LANES : (h + 1) * LANES], HALF, 1) for h in range(heads)], axis=1
        )

    for b, block in enumerate(blocks):
        r = slice(b * rows, (b + 1) * rows)
        places = block[rows:, :rows].astype(f32)
        seg_r[:, r] = places[0:1, :]
        columns = places.T
        seg_c[r, :] = columns[:, 0:1]
        rows_at = lax.broadcasted_iota(jnp.int32, (rows, ROW_LIMIT), 1).astype(f32)
        cols_at = lax.broadcasted_iota(jnp.int32, (rows, COL_LIMIT), 1).astype(f32)
        hot_r = (columns[:, 1:2] == rows_at).astype(bf16)
        hot_c = (columns[:, 2:3] == cols_at).astype(bf16)
        cos_b = jnp.zeros((rows, LANES), f32)
        sin_b = jnp.zeros((rows, LANES), f32)
        for piece in range(3):
            found = dot_nn(hot_r, table_r_ref[piece]) + dot_nn(hot_c, table_c_ref[piece])
            cos_b += found[:, :LANES]
            sin_b += found[:, LANES:]
        cos_t[r, :] = cos_b
        sin_t[r, :] = sin_b
        if b % 4 == 0:
            four = jnp.concatenate([x[:rows, :] for x in blocks[b : b + 4]], axis=0)
            joined = dot_nn(four, w_ref[...])
        qkv = joined[b % 4 * rows : (b % 4 + 1) * rows, :]
        cos2 = jnp.concatenate([cos_b] * heads, axis=1)
        sin2 = jnp.concatenate([sin_b] * heads, axis=1)
        qu = qkv[:, :padded]
        ku = qkv[:, padded : 2 * padded]
        q[r, :] = ((qu * cos2 + halves(qu) * sin2) * (scale * LOG2E)).astype(bf16)
        k[r, :] = (ku * cos2 + halves(ku) * sin2).astype(bf16)
        v[r, :] = jnp.where(lane == ONE_LANE, 1.0, qkv[:, 2 * padded :]).astype(bf16)
        packed = gm_ref[at_ref[b]]
        part = packed.shape[0]
        for i in range(rows // part):
            piece = packed[:, i * own : (i + 1) * own]
            start = b * rows + i * part
            g[start : start + part, :] = dot_nn(piece, spread_ref[...]).astype(bf16)

    for h in range(heads):
        c = slice(h * LANES, (h + 1) * LANES)
        kt[h] = k[:, c].T
        vt[h] = v[:, c].T
    dk[...] = jnp.zeros_like(dk)
    dv[...] = jnp.zeros_like(dv)
    segk = seg_c[...]

    def turn_back(x, start):
        r = pl.ds(start, x.shape[0])
        return x * cos_t[r, :] - pltpu.roll(x, HALF, 1) * sin_t[r, :]

    def step(i, carry):
        start = pl.multiple_of(i * BLOCK_Q, BLOCK_Q)
        r = pl.ds(start, BLOCK_Q)
        same = segk == seg_r[:, r]
        lanes = [slice(h * LANES, (h + 1) * LANES) for h in range(heads)]
        qb = [q[r, c] for c in lanes]
        gb = [g[r, c] for c in lanes]

        def weights(h):
            st = jnp.where(same, dot_nt(k[:, lanes[h]], qb[h]), -jnp.inf)
            return jnp.exp2(st - jnp.max(st, axis=0, keepdims=True)).astype(bf16)

        def forward(h, e):
            ot = dot_nn(vt[h], e)
            o = ot.T
            inv_col = 1.0 / o[:, ONE_LANE : ONE_LANE + 1]
            inv_row = 1.0 / ot[ONE_LANE : ONE_LANE + 1, :]
            mixed_pad[r, lanes[h]] = (o * inv_col).astype(bf16)
            centre = jnp.sum(gb[h].astype(f32).T * ot, axis=0, keepdims=True) * inv_row
            dv[h] += dot_nn(e, (gb[h].astype(f32) * inv_col).astype(bf16))
            return inv_col, inv_row, centre

        def backward(h, e, inv_col, inv_row, centre):
            dst = e * (dot_nt(v[:, lanes[h]], gb[h]) - centre).astype(bf16)
            dqt = dot_nn(kt[h], dst) * (inv_row * scale)
            dq_pad[r, lanes[h]] = turn_back(dqt.T, start).astype(bf16)
            dk[h] += dot_nn(dst, (qb[h].astype(f32) * inv_col).astype(bf16))

        before = None
        for h in range(heads):
            e = weights(h)
            if before is not None:
                backward(*before)
            before = (h, e, *forward(h, e))
        backward(*before)
        return carry

    lax.fori_loop(0, length // BLOCK_Q, step, 0)

    for b in range(len(blocks)):
        start = b * rows
        r = slice(start, start + rows)
        pick = pick_ref[...]
        dk_pad = [turn_back(dk[h, r, :] * (1 / LOG2E), start).astype(bf16) for h in range(heads)]
        dv_pad = [dv[h, r, :].astype(bf16) for h in range(heads)]
        grads = [dq_pad[r, :], jnp.concatenate(dk_pad, axis=1), jnp.concatenate(dv_pad, axis=1)]
        grads = jnp.concatenate([dot_nn(p, pick) for p in grads], axis=1)
        mixed = dot_nn(mixed_pad[r, :], pick)
        mixed_ref[r, :] = mixed.astype(bf16)
        outs[b % 4][b // 4] = jnp.concatenate([mixed, grads], axis=1).astype(bf16)
        grads_all[r, :] = grads.astype(bf16)

    term = None
    half = len(blocks) // 2
    for first in (0, half):
        lefts = jnp.concatenate([block[:rows, :] for block in blocks[first : first + half]], axis=0)
        part = dot_tn(lefts, grads_all[first * rows : (first + half) * rows, :])
        term = part if term is None else term + part
    term_ref[...] = term.astype(bf16)


def attend(at, blocks, gm, w_own, table_r, table_c, pick, spread):
    rows = blocks[0].shape[0] - EXTRA
    length = rows * len(blocks)
    padded, own = pick.shape
    heads = padded // LANES
    return pl.pallas_call(
        attend_kernel,
        out_shape=[jax.ShapeDtypeStruct((2, rows, 4 * own), bf16) for _ in range(4)]
        + [jax.ShapeDtypeStruct((blocks[0].shape[1], 3 * own), bf16)]
        + [jax.ShapeDtypeStruct((length, own), bf16)],
        in_specs=[SMEM] + [VMEM] * (len(blocks) + 6),
        out_specs=[VMEM] * 6,
        scratch_shapes=[pltpu.VMEM((length, padded), bf16) for _ in range(4)]
        + [pltpu.VMEM((heads, LANES, length), bf16) for _ in range(2)]
        + [pltpu.VMEM((heads, length, LANES), f32) for _ in range(2)]
        + [pltpu.VMEM((length, padded), bf16) for _ in range(2)]
        + [pltpu.VMEM((length, LANES), f32) for _ in range(2)]
        + [pltpu.VMEM((length, 1), f32), pltpu.VMEM((1, length), f32)]
        + [pltpu.VMEM((length, 3 * own), bf16)],
        compiler_params=params(58),
        cost_estimate=cost(
            12 * heads * length * length * LANES + 2 * length * blocks[0].shape[1] * w_own.shape[1],
            length * blocks[0].shape[1] * 4,
            heads * length * length,
        ),
    )(at, *blocks, gm, w_own, table_r, table_c, pick, spread)


def weight_out_kernel(
    mixed_hbm, term_hbm, move_hbm, c0, c1, c2, c3, c7, out_ref, mixed, term, move, held, sems
):
    n = held.shape[0]
    copies = [pltpu.make_async_copy(mixed_hbm, mixed, sems.at[0])]
    for i in range(n):
        source = (c3, c7)[i // 4] if i % 4 == 3 else (c0, c1, c2)[i % 4].at[i // 4]
        copies.append(pltpu.make_async_copy(source, held.at[i], sems.at[i + 1]))
    copies.append(pltpu.make_async_copy(move_hbm, move, sems.at[n + 1]))
    copies.append(pltpu.make_async_copy(term_hbm, term, sems.at[n + 2]))
    for copy in copies:
        copy.start()
    copies[0].wait()
    n_dp, chunk, _ = out_ref.shape
    rows = held.shape[1]
    own = mixed.shape[1]
    total = None
    for i in range(n):
        copies[i + 1].wait()
        part = dot_tn(mixed[i * rows : (i + 1) * rows, :], held[i])
        total = part if total is None else total + part
    total = total.astype(bf16)
    groups = total.shape[1] // own
    copies[n + 1].wait()
    moved = []
    part = move.shape[0] // groups
    for first in range(0, own, part):
        top = total[first : first + part, :]
        stacked = [top[:, i * own : (i + 1) * own] for i in range(groups)]
        moved.append(dot_nn(move[...], jnp.concatenate(stacked, axis=0)).astype(bf16))
    moved = jnp.concatenate(moved, axis=0)
    copies[n + 2].wait()
    for j in range(n_dp):
        r = slice(j * chunk, (j + 1) * chunk)
        out_ref[j] = jnp.concatenate([term[r, :], moved[r, :]], axis=1)


def weight_terms(mixed, term_qkv, move, cots, n_dp):
    _, rows, width = cots[0].shape
    length, own = mixed.shape
    chunk = width // n_dp
    n = length // rows
    return pl.pallas_call(
        weight_out_kernel,
        out_shape=jax.ShapeDtypeStruct((n_dp, chunk, 4 * own), bf16),
        in_specs=[ANY] * (len(cots) + 3),
        out_specs=VMEM,
        scratch_shapes=[
            pltpu.VMEM(mixed.shape, bf16),
            pltpu.VMEM(term_qkv.shape, bf16),
            pltpu.VMEM(move.shape, bf16),
            pltpu.VMEM((n, rows, width), bf16),
            pltpu.SemaphoreType.DMA((n + 3,)),
        ],
        compiler_params=params(60),
        cost_estimate=cost(2 * length * width * own, length * width * 3),
    )(mixed, term_qkv, move, *cots)


def sum_kernel(factor, own, in_ref, qkv_ref, out_ref):
    total = in_ref[0].astype(f32)
    for i in range(1, in_ref.shape[0]):
        total += in_ref[i].astype(f32)
    total = total * factor
    size, part, columns = qkv_ref.shape
    for s in range(size):
        piece = total[s * part : (s + 1) * part, :]
        qkv_ref[s] = piece[:, :columns]
        out_ref[:, s * own : (s + 1) * own] = piece[:, columns:]


def sum_terms(terms, size, own, factor):
    n_dp, chunk, columns = terms.shape
    part = chunk // size
    return pl.pallas_call(
        functools.partial(sum_kernel, factor, own),
        out_shape=[
            jax.ShapeDtypeStruct((size, part, columns - own), f32),
            jax.ShapeDtypeStruct((part, size * own), f32),
        ],
        in_specs=[VMEM],
        out_specs=[VMEM] * 2,
        compiler_params=params(32),
        cost_estimate=cost(n_dp * chunk * columns, 2 * n_dp * chunk * columns),
    )(terms)


def place_kernel(in_ref, w_ref, gain_ref, qkv_ref, gain_out_ref):
    size, _, columns = in_ref.shape
    own = columns // 3
    for t in range(3):
        for s in range(size):
            start = t * size * own + s * own
            qkv_ref[:, start : start + own] = in_ref[s][:, t * own : (t + 1) * own]
    gain_out_ref[...] = jnp.sum(qkv_ref[...] * w_ref[...], axis=1) / gain_ref[...]


def place(parts, w_rows, gain_rows):
    size, rows, columns = parts.shape
    return pl.pallas_call(
        place_kernel,
        out_shape=[
            jax.ShapeDtypeStruct((rows, size * columns), f32),
            jax.ShapeDtypeStruct((rows,), f32),
        ],
        in_specs=[VMEM] * 3,
        out_specs=[VMEM] * 2,
        cost_estimate=cost(2 * rows * size * columns, 12 * rows * size * columns),
    )(parts, w_rows, gain_rows)


def finish_kernel(
    from_ref, p0, p1, p2, p3, c0, c1, c2, c3, w_qkv_hbm, w_out_hbm, tok_hbm, cot_hbm, gain_ref,
    result_ref, grad_ref, held, weights, sides, rows_in, sems,
):
    size = held.shape[0]
    width = rows_in.shape[2]
    own = width // size
    blocks = [p0.at[0], p1.at[0], p2.at[0], p3.at[0], c0, c1, c2, c3]
    sources = [w_out_hbm] + [w_qkv_hbm.at[:, pl.ds(t * width, width)] for t in range(3)]
    copies = [pltpu.make_async_copy(b, held.at[i], sems.at[i]) for i, b in enumerate(blocks)]
    loads = [
        pltpu.make_async_copy(w, weights.at[i], sems.at[size + i]) for i, w in enumerate(sources)
    ]
    tok_copy = pltpu.make_async_copy(tok_hbm, rows_in.at[0], sems.at[size + 4])
    cot_copy = pltpu.make_async_copy(cot_hbm, rows_in.at[1], sems.at[size + 5])
    for copy in copies + loads[:1] + [tok_copy] + loads[1:] + [cot_copy]:
        copy.start()
    for copy in copies:
        copy.wait()
    for kind in range(4):
        parts = [held[from_ref[s], :, kind * own : (kind + 1) * own] for s in range(size)]
        sides[kind] = jnp.concatenate(parts, axis=1)
    loads[0].wait()
    tok_copy.wait()
    wide = rows_in[0].astype(f32)
    result_ref[...] = (wide + dot_nn(sides[0], weights[0])).astype(bf16)
    loads[1].wait()
    total = dot_nt(sides[1], weights[1])
    for kind in (2, 3):
        loads[kind].wait()
        total += dot_nt(sides[kind], weights[kind])
    inverse = lax.rsqrt(jnp.mean(wide * wide, axis=-1, keepdims=True) + NORM_EPSILON)
    pre_gain = total * gain_ref[...][None, :]
    inner = jnp.mean(pre_gain * wide, axis=-1, keepdims=True)
    grad_x = inverse * pre_gain - (inverse * inverse * inverse) * wide * inner
    cot_copy.wait()
    grad_ref[...] = (rows_in[1].astype(f32) + grad_x).astype(bf16)


def finish(source, pairs, cross, tokens, cotangent, gain, w_qkv, w_out):
    rows, width = tokens.shape
    n = len(pairs) + len(cross)
    out = jax.ShapeDtypeStruct((rows, width), bf16)
    return pl.pallas_call(
        finish_kernel,
        out_shape=[out, out],
        in_specs=[SMEM] + [ANY] * (n + 4) + [VMEM],
        out_specs=[VMEM] * 2,
        scratch_shapes=[
            pltpu.VMEM((n,) + cross[0].shape, bf16),
            pltpu.VMEM((4, width, width), bf16),
            pltpu.VMEM((4, rows, width), bf16),
            pltpu.VMEM((2, rows, width), bf16),
            pltpu.SemaphoreType.DMA((n + 6,)),
        ],
        compiler_params=params(60),
        cost_estimate=cost(32 * rows * width * width, 8 * width * width),
    )(source, *pairs, *cross, w_qkv, w_out, tokens, cotangent, gain)


def split3(table):
    first = table.astype(bf16)
    rest = table - first.astype(f32)
    second = rest.astype(bf16)
    third = (rest - second.astype(f32)).astype(bf16)
    return jnp.stack([first, second, third])


def rope_lookup(head_size):
    quarter = head_size // 4
    frequency = ROPE_BASE ** (-jnp.arange(quarter, dtype=f32) / quarter)

    def spread(limit, first):
        angles = jnp.arange(limit, dtype=f32)[:, None] * frequency
        cos, sin = jnp.cos(angles), jnp.sin(angles)
        none = jnp.zeros_like(cos)
        gap = jnp.zeros((limit, HALF - 2 * quarter), f32)
        pair = (lambda x: [x, none, gap]) if first else (lambda x: [none, x, gap])
        return jnp.concatenate(pair(cos) * 2 + pair(-sin) + pair(sin), axis=1)

    return split3(spread(ROW_LIMIT, True)), split3(spread(COL_LIMIT, False))


def gather(value, size):
    return [value] + [shift(value, OFFSETS[MIRROR[b]], size) for b in (1, 2, 3)]


def local(tokens, norm_gain, w_qkv, w_out, cotangent, segment, patch_row, patch_col):
    rows, width = tokens.shape
    size = lax.axis_size("seq")
    n_dp = lax.axis_size("dp")
    me = lax.axis_index("seq")
    head_size = width // HEADS
    own = HEADS // size * head_size
    padded = HEADS // size * LANES
    at = [((me // 2 + dz) % (size // 2)) * 2 + ((me % 2) ^ dc) for dz, dc in OFFSETS]
    at = jnp.stack(at).astype(jnp.int32)
    every = jnp.arange(size)
    steps = (every // 2 - me // 2) % (size // 2)
    source_of = jnp.where(steps == 0, 0, jnp.where(steps == size // 2 - 1, 1, steps + 1))
    source_of = (source_of + size // 2 * ((every % 2) ^ (me % 2))).astype(jnp.int32)

    payload = normalise(tokens, norm_gain, segment, patch_row, patch_col)
    mine = gather(payload, size)
    own_swap = shift(payload, (0, 1), size)
    cot_pair = jnp.stack([cotangent, shift(cotangent, (0, 1), size)])
    blocks = mine + [own_swap] + [shift(m, (0, 1), size) for m in mine[1:]]
    gm = grad_mixed_blocks(cotangent, w_out, size)
    gm = lax.all_to_all(gm, "seq", split_axis=0, concat_axis=0, tiled=True)

    lane = jnp.arange(padded)
    within = lane % HALF
    source = (lane // LANES) * head_size + (lane % LANES) // HALF * (head_size // 2) + within
    used = within < head_size // 2
    pick = ((source[:, None] == jnp.arange(own)[None, :]) & used[:, None]).astype(bf16)
    expand = ((source[None, :] == jnp.arange(own)[:, None]) & used[None, :]).astype(bf16)
    spread = ((source + me * own)[None, :] == jnp.arange(width)[:, None]) & used[None, :]
    spread = spread.astype(bf16)
    w_own = jnp.concatenate(
        [dot_nn(w_qkv[:, t * width : (t + 1) * width], spread).astype(bf16) for t in range(3)],
        axis=1,
    )
    table_r, table_c = rope_lookup(head_size)

    chunk = width // n_dp
    out_rows = chunk // size
    half_rows = own // 2
    row = jnp.arange(width // 2)
    moved_from = (row % chunk) // out_rows * half_rows + row // chunk * out_rows + row % out_rows
    move = (moved_from[:, None] == row[None, :]).astype(bf16)
    cot_pair, cot, _ = lax.optimization_barrier((cot_pair, cotangent, (mine[1:], own_swap)))
    cots = [cot_pair] + [shift(cot_pair, OFFSETS[MIRROR[b]], size) for b in (1, 2)]
    cots.append(shift(cot, OFFSETS[MIRROR[3]], size))
    w_own, move = lax.optimization_barrier((w_own, move))
    *attended, term_qkv, mixed = attend(at, blocks, gm, w_own, table_r, table_c, pick, expand)
    cots, attended = lax.optimization_barrier((cots, attended))
    cots.append(shift(cots[3], (0, 1), size))

    pairs = [attended[0]] + [None] * 3
    for b in (1, 2, 3):
        pairs[MIRROR[b]] = shift(attended[b], OFFSETS[b], size)

    terms = weight_terms(mixed, term_qkv, move, cots, n_dp)
    first = (lax.axis_index("dp") * size + me) * out_rows
    first, _ = lax.optimization_barrier((first, terms))
    pairs, _ = lax.optimization_barrier((pairs, terms))
    w_rows = lax.dynamic_slice(w_qkv, (first, 0), (out_rows, 3 * width)).astype(f32)
    gain_rows = lax.dynamic_slice(norm_gain, (first,), (out_rows,))
    cross = [shift(pair[1], (0, 1), size) for pair in pairs]
    terms = lax.all_to_all(terms, "dp", split_axis=0, concat_axis=0, tiled=True)
    result, grad_tokens = finish(
        source_of, pairs, cross, tokens, cotangent, norm_gain, w_qkv, w_out
    )

    factor = float(rows * size * n_dp) ** (-0.5)
    part_qkv, part_out = sum_terms(terms, size, own, factor)
    part_qkv = lax.all_to_all(part_qkv, "seq", split_axis=0, concat_axis=0, tiled=True)
    pairs = [(j * size + s, s * n_dp + j) for j in range(n_dp) for s in range(size)]
    grad_out = lax.ppermute(part_out, ("dp", "seq"), pairs)
    grad_qkv, grad_gain = place(part_qkv, w_rows, gain_rows)
    return (result, grad_tokens, grad_qkv, grad_out, grad_gain)


def solution(mesh):
    both = P(("dp", "seq"), None)
    flat = P(("dp", "seq"))
    return jax.shard_map(
        local,
        mesh=mesh,
        in_specs=(both, P(), P(), P(), both, flat, flat, flat),
        out_specs=(both, both, both, both, flat),
        check_vma=False,
    )
```

```python
import functools

import jax
import jax.numpy as jnp
from jax import lax
from jax.experimental import pallas as pl
from jax.experimental.pallas import tpu as pltpu
from jax.sharding import PartitionSpec as P

HEADS = 16
NORM_EPSILON = 1e-06
ROPE_BASE = 10000.0
LOG2E = 1.4426950408889634
LANES = 128
HALF = 64
ONE_LANE = 40
BLOCK_Q = 1024
ROW_LIMIT = 256
COL_LIMIT = 128
EXTRA = 16

bf16 = jnp.bfloat16
f32 = jnp.float32

OFFSETS = ((0, 0), (-1, 0), (1, 0), (2, 0), (0, 1), (-1, 1), (1, 1), (2, 1))
MIRROR = (0, 2, 1, 3, 4, 6, 5, 7)
VMEM = pl.BlockSpec(memory_space=pltpu.VMEM)
SMEM = pl.BlockSpec(memory_space=pltpu.SMEM)
ANY = pl.BlockSpec(memory_space=pl.ANY)


def dot_nt(a, b):
    return lax.dot_general(a, b, (((1,), (1,)), ((), ())), preferred_element_type=f32)


def dot_nn(a, b):
    return lax.dot_general(a, b, (((1,), (0,)), ((), ())), preferred_element_type=f32)


def dot_tn(a, b):
    return lax.dot_general(a, b, (((0,), (0,)), ((), ())), preferred_element_type=f32)


def shift(value, offset, size):
    dz, dc = offset
    depth = size // 2
    pairs = [(i, ((i // 2 + dz) % depth) * 2 + ((i % 2) ^ dc)) for i in range(size)]
    return lax.ppermute(value, "seq", pairs)


def params(mib):
    return pltpu.CompilerParams(vmem_limit_bytes=mib * 2**20)


def cost(flops, nbytes, exps=0):
    return pl.CostEstimate(flops=flops, bytes_accessed=nbytes, transcendentals=exps)


def norm_kernel(tok_ref, gain_ref, seg_ref, row_ref, col_ref, out_ref):
    rows = tok_ref.shape[0]
    wide = tok_ref[...].astype(f32)
    inverse = lax.rsqrt(jnp.mean(wide * wide, axis=-1, keepdims=True) + NORM_EPSILON)
    out_ref[:rows, :] = (wide * inverse * gain_ref[...][None, :]).astype(bf16)
    out_ref[rows:, :] = jnp.zeros((EXTRA, out_ref.shape[1]), bf16)
    places = [r[...][None, :].astype(f32) for r in (seg_ref, row_ref, col_ref)]
    places.append(jnp.zeros((EXTRA - 3, rows), f32))
    out_ref[rows:, :rows] = jnp.concatenate(places, axis=0).astype(bf16)


def normalise(tokens, gain, segment, patch_row, patch_col):
    rows, width = tokens.shape
    return pl.pallas_call(
        norm_kernel,
        out_shape=jax.ShapeDtypeStruct((rows + EXTRA, width), bf16),
        in_specs=[VMEM] * 5,
        out_specs=VMEM,
        cost_estimate=cost(8 * rows * width, 4 * rows * width),
    )(tokens, gain, segment, patch_row, patch_col)


def grad_mixed_kernel(cot_ref, w_ref, out_ref):
    size, part, lanes = out_ref.shape
    grad = dot_nt(cot_ref[...], w_ref[...])
    own = w_ref.shape[0] // size
    for s in range(size):
        pieces = [
            grad[i * part : (i + 1) * part, s * own : (s + 1) * own] for i in range(lanes // own)
        ]
        out_ref[s] = jnp.concatenate(pieces, axis=1).astype(bf16)


def grad_mixed_blocks(cotangent, w_out, size):
    rows, width = cotangent.shape
    return pl.pallas_call(
        grad_mixed_kernel,
        out_shape=jax.ShapeDtypeStruct((size, rows // 4, 4 * width // size), bf16),
        in_specs=[VMEM] * 2,
        out_specs=VMEM,
        compiler_params=params(32),
        cost_estimate=cost(2 * rows * width * width, 2 * width * width),
    )(cotangent, w_out)


def attend_kernel(*refs):
    at_ref = refs[0]
    blocks = refs[1:9]
    gm_ref, w_ref, table_r_ref, table_c_ref, pick_ref, spread_ref = refs[9:15]
    outs = refs[15:19]
    term_ref, mixed_ref = refs[19:21]
    q, k, v, g, kt, vt, dk, dv, mixed_pad, dq_pad, cos_t, sin_t, seg_c, seg_r, grads_all = refs[21:]
    length, padded = q.shape
    heads = padded // LANES
    rows = length // len(blocks)
    own = pick_ref.shape[1]
    scale = 80.0**-0.5
    lane = lax.broadcasted_iota(jnp.int32, (1, padded), 1) % LANES

    def halves(u):
        return jnp.concatenate(
            [pltpu.roll(u[:, h * LANES : (h + 1) * LANES], HALF, 1) for h in range(heads)], axis=1
        )

    for b, block in enumerate(blocks):
        r = slice(b * rows, (b + 1) * rows)
        places = block[rows:, :rows].astype(f32)
        seg_r[:, r] = places[0:1, :]
        columns = places.T
        seg_c[r, :] = columns[:, 0:1]
        rows_at = lax.broadcasted_iota(jnp.int32, (rows, ROW_LIMIT), 1).astype(f32)
        cols_at = lax.broadcasted_iota(jnp.int32, (rows, COL_LIMIT), 1).astype(f32)
        hot_r = (columns[:, 1:2] == rows_at).astype(bf16)
        hot_c = (columns[:, 2:3] == cols_at).astype(bf16)
        cos_b = jnp.zeros((rows, LANES), f32)
        sin_b = jnp.zeros((rows, LANES), f32)
        for piece in range(3):
            found = dot_nn(hot_r, table_r_ref[piece]) + dot_nn(hot_c, table_c_ref[piece])
            cos_b += found[:, :LANES]
            sin_b += found[:, LANES:]
        cos_t[r, :] = cos_b
        sin_t[r, :] = sin_b
        qkv = dot_nn(block[:rows, :], w_ref[...])
        cos2 = jnp.concatenate([cos_b] * heads, axis=1)
        sin2 = jnp.concatenate([sin_b] * heads, axis=1)
        qu = qkv[:, :padded]
        ku = qkv[:, padded : 2 * padded]
        q[r, :] = ((qu * cos2 + halves(qu) * sin2) * (scale * LOG2E)).astype(bf16)
        k[r, :] = (ku * cos2 + halves(ku) * sin2).astype(bf16)
        v[r, :] = jnp.where(lane == ONE_LANE, 1.0, qkv[:, 2 * padded :]).astype(bf16)
        packed = gm_ref[at_ref[b]]
        part = packed.shape[0]
        for i in range(rows // part):
            piece = packed[:, i * own : (i + 1) * own]
            start = b * rows + i * part
            g[start : start + part, :] = dot_nn(piece, spread_ref[...]).astype(bf16)

    for h in range(heads):
        c = slice(h * LANES, (h + 1) * LANES)
        kt[h] = k[:, c].T
        vt[h] = v[:, c].T
    dk[...] = jnp.zeros_like(dk)
    dv[...] = jnp.zeros_like(dv)
    segk = seg_c[...]

    def turn_back(x, start):
        r = pl.ds(start, x.shape[0])
        return x * cos_t[r, :] - pltpu.roll(x, HALF, 1) * sin_t[r, :]

    def step(i, carry):
        start = pl.multiple_of(i * BLOCK_Q, BLOCK_Q)
        r = pl.ds(start, BLOCK_Q)
        same = segk == seg_r[:, r]
        lanes = [slice(h * LANES, (h + 1) * LANES) for h in range(heads)]
        qb = [q[r, c] for c in lanes]
        gb = [g[r, c] for c in lanes]

        def weights(h):
            st = jnp.where(same, dot_nt(k[:, lanes[h]], qb[h]), -jnp.inf)
            return jnp.exp2(st - jnp.max(st, axis=0, keepdims=True)).astype(bf16)

        def forward(h, e):
            ot = dot_nn(vt[h], e)
            o = ot.T
            inv_col = 1.0 / o[:, ONE_LANE : ONE_LANE + 1]
            inv_row = 1.0 / ot[ONE_LANE : ONE_LANE + 1, :]
            mixed_pad[r, lanes[h]] = (o * inv_col).astype(bf16)
            centre = jnp.sum(gb[h].astype(f32).T * ot, axis=0, keepdims=True) * inv_row
            dv[h] += dot_nn(e, (gb[h].astype(f32) * inv_col).astype(bf16))
            return inv_col, inv_row, centre

        def backward(h, e, inv_col, inv_row, centre):
            dst = e * (dot_nt(v[:, lanes[h]], gb[h]) - centre).astype(bf16)
            dqt = dot_nn(kt[h], dst) * (inv_row * scale)
            dq_pad[r, lanes[h]] = turn_back(dqt.T, start).astype(bf16)
            dk[h] += dot_nn(dst, (qb[h].astype(f32) * inv_col).astype(bf16))

        before = None
        for h in range(heads):
            e = weights(h)
            if before is not None:
                backward(*before)
            before = (h, e, *forward(h, e))
        backward(*before)
        return carry

    lax.fori_loop(0, length // BLOCK_Q, step, 0)

    for b in range(len(blocks)):
        start = b * rows
        r = slice(start, start + rows)
        pick = pick_ref[...]
        dk_pad = [turn_back(dk[h, r, :] * (1 / LOG2E), start).astype(bf16) for h in range(heads)]
        dv_pad = [dv[h, r, :].astype(bf16) for h in range(heads)]
        grads = [dq_pad[r, :], jnp.concatenate(dk_pad, axis=1), jnp.concatenate(dv_pad, axis=1)]
        grads = jnp.concatenate([dot_nn(p, pick) for p in grads], axis=1)
        mixed = dot_nn(mixed_pad[r, :], pick)
        mixed_ref[r, :] = mixed.astype(bf16)
        outs[b % 4][b // 4] = jnp.concatenate([mixed, grads], axis=1).astype(bf16)
        grads_all[r, :] = grads.astype(bf16)

    term = None
    half = len(blocks) // 2
    for first in (0, half):
        lefts = jnp.concatenate([block[:rows, :] for block in blocks[first : first + half]], axis=0)
        part = dot_tn(lefts, grads_all[first * rows : (first + half) * rows, :])
        term = part if term is None else term + part
    term_ref[...] = term.astype(bf16)


def attend(at, blocks, gm, w_own, table_r, table_c, pick, spread):
    rows = blocks[0].shape[0] - EXTRA
    length = rows * len(blocks)
    padded, own = pick.shape
    heads = padded // LANES
    return pl.pallas_call(
        attend_kernel,
        out_shape=[jax.ShapeDtypeStruct((2, rows, 4 * own), bf16) for _ in range(4)]
        + [jax.ShapeDtypeStruct((blocks[0].shape[1], 3 * own), bf16)]
        + [jax.ShapeDtypeStruct((length, own), bf16)],
        in_specs=[SMEM] + [VMEM] * (len(blocks) + 6),
        out_specs=[VMEM] * 6,
        scratch_shapes=[pltpu.VMEM((length, padded), bf16) for _ in range(4)]
        + [pltpu.VMEM((heads, LANES, length), bf16) for _ in range(2)]
        + [pltpu.VMEM((heads, length, LANES), f32) for _ in range(2)]
        + [pltpu.VMEM((length, padded), bf16) for _ in range(2)]
        + [pltpu.VMEM((length, LANES), f32) for _ in range(2)]
        + [pltpu.VMEM((length, 1), f32), pltpu.VMEM((1, length), f32)]
        + [pltpu.VMEM((length, 3 * own), bf16)],
        compiler_params=params(58),
        cost_estimate=cost(
            12 * heads * length * length * LANES + 2 * length * blocks[0].shape[1] * w_own.shape[1],
            length * blocks[0].shape[1] * 4,
            heads * length * length,
        ),
    )(at, *blocks, gm, w_own, table_r, table_c, pick, spread)


def weight_out_kernel(
    mixed_hbm, term_hbm, move_hbm, c0, c1, c2, c3, c7, out_ref, mixed, term, move, held, sems
):
    n = held.shape[0]
    copies = [pltpu.make_async_copy(mixed_hbm, mixed, sems.at[0])]
    for i in range(n):
        source = (c3, c7)[i // 4] if i % 4 == 3 else (c0, c1, c2)[i % 4].at[i // 4]
        copies.append(pltpu.make_async_copy(source, held.at[i], sems.at[i + 1]))
    copies.append(pltpu.make_async_copy(move_hbm, move, sems.at[n + 1]))
    copies.append(pltpu.make_async_copy(term_hbm, term, sems.at[n + 2]))
    for copy in copies:
        copy.start()
    copies[0].wait()
    n_dp, chunk, _ = out_ref.shape
    rows = held.shape[1]
    own = mixed.shape[1]
    total = None
    for i in range(n):
        copies[i + 1].wait()
        part = dot_tn(mixed[i * rows : (i + 1) * rows, :], held[i])
        total = part if total is None else total + part
    total = total.astype(bf16)
    groups = total.shape[1] // own
    copies[n + 1].wait()
    moved = []
    part = move.shape[0] // groups
    for first in range(0, own, part):
        top = total[first : first + part, :]
        stacked = [top[:, i * own : (i + 1) * own] for i in range(groups)]
        moved.append(dot_nn(move[...], jnp.concatenate(stacked, axis=0)).astype(bf16))
    moved = jnp.concatenate(moved, axis=0)
    copies[n + 2].wait()
    for j in range(n_dp):
        r = slice(j * chunk, (j + 1) * chunk)
        out_ref[j] = jnp.concatenate([term[r, :], moved[r, :]], axis=1)


def weight_terms(mixed, term_qkv, move, cots, n_dp):
    _, rows, width = cots[0].shape
    length, own = mixed.shape
    chunk = width // n_dp
    n = length // rows
    return pl.pallas_call(
        weight_out_kernel,
        out_shape=jax.ShapeDtypeStruct((n_dp, chunk, 4 * own), bf16),
        in_specs=[ANY] * (len(cots) + 3),
        out_specs=VMEM,
        scratch_shapes=[
            pltpu.VMEM(mixed.shape, bf16),
            pltpu.VMEM(term_qkv.shape, bf16),
            pltpu.VMEM(move.shape, bf16),
            pltpu.VMEM((n, rows, width), bf16),
            pltpu.SemaphoreType.DMA((n + 3,)),
        ],
        compiler_params=params(60),
        cost_estimate=cost(2 * length * width * own, length * width * 3),
    )(mixed, term_qkv, move, *cots)


def sum_kernel(factor, own, in_ref, qkv_ref, out_ref):
    total = in_ref[0].astype(f32)
    for i in range(1, in_ref.shape[0]):
        total += in_ref[i].astype(f32)
    total = total * factor
    size, part, columns = qkv_ref.shape
    for s in range(size):
        piece = total[s * part : (s + 1) * part, :]
        qkv_ref[s] = piece[:, :columns]
        out_ref[:, s * own : (s + 1) * own] = piece[:, columns:]


def sum_terms(terms, size, own, factor):
    n_dp, chunk, columns = terms.shape
    part = chunk // size
    return pl.pallas_call(
        functools.partial(sum_kernel, factor, own),
        out_shape=[
            jax.ShapeDtypeStruct((size, part, columns - own), f32),
            jax.ShapeDtypeStruct((part, size * own), f32),
        ],
        in_specs=[VMEM],
        out_specs=[VMEM] * 2,
        compiler_params=params(32),
        cost_estimate=cost(n_dp * chunk * columns, 2 * n_dp * chunk * columns),
    )(terms)


def place_kernel(in_ref, w_ref, gain_ref, qkv_ref, gain_out_ref):
    size, _, columns = in_ref.shape
    own = columns // 3
    for t in range(3):
        for s in range(size):
            start = t * size * own + s * own
            qkv_ref[:, start : start + own] = in_ref[s][:, t * own : (t + 1) * own]
    gain_out_ref[...] = jnp.sum(qkv_ref[...] * w_ref[...], axis=1) / gain_ref[...]


def place(parts, w_rows, gain_rows):
    size, rows, columns = parts.shape
    return pl.pallas_call(
        place_kernel,
        out_shape=[
            jax.ShapeDtypeStruct((rows, size * columns), f32),
            jax.ShapeDtypeStruct((rows,), f32),
        ],
        in_specs=[VMEM] * 3,
        out_specs=[VMEM] * 2,
        cost_estimate=cost(2 * rows * size * columns, 12 * rows * size * columns),
    )(parts, w_rows, gain_rows)


def finish_kernel(
    from_ref, p0, p1, p2, p3, c0, c1, c2, c3, w_qkv_hbm, w_out_hbm, tok_hbm, cot_hbm, gain_ref,
    result_ref, grad_ref, held, weights, sides, rows_in, sems,
):
    size = held.shape[0]
    width = rows_in.shape[2]
    own = width // size
    blocks = [p0.at[0], p1.at[0], p2.at[0], p3.at[0], c0, c1, c2, c3]
    sources = [w_out_hbm] + [w_qkv_hbm.at[:, pl.ds(t * width, width)] for t in range(3)]
    copies = [pltpu.make_async_copy(b, held.at[i], sems.at[i]) for i, b in enumerate(blocks)]
    loads = [
        pltpu.make_async_copy(w, weights.at[i], sems.at[size + i]) for i, w in enumerate(sources)
    ]
    tok_copy = pltpu.make_async_copy(tok_hbm, rows_in.at[0], sems.at[size + 4])
    cot_copy = pltpu.make_async_copy(cot_hbm, rows_in.at[1], sems.at[size + 5])
    for copy in copies + loads[:1] + [tok_copy] + loads[1:] + [cot_copy]:
        copy.start()
    for copy in copies:
        copy.wait()
    for kind in range(4):
        parts = [held[from_ref[s], :, kind * own : (kind + 1) * own] for s in range(size)]
        sides[kind] = jnp.concatenate(parts, axis=1)
    loads[0].wait()
    tok_copy.wait()
    wide = rows_in[0].astype(f32)
    result_ref[...] = (wide + dot_nn(sides[0], weights[0])).astype(bf16)
    loads[1].wait()
    total = dot_nt(sides[1], weights[1])
    for kind in (2, 3):
        loads[kind].wait()
        total += dot_nt(sides[kind], weights[kind])
    inverse = lax.rsqrt(jnp.mean(wide * wide, axis=-1, keepdims=True) + NORM_EPSILON)
    pre_gain = total * gain_ref[...][None, :]
    inner = jnp.mean(pre_gain * wide, axis=-1, keepdims=True)
    grad_x = inverse * pre_gain - (inverse * inverse * inverse) * wide * inner
    cot_copy.wait()
    grad_ref[...] = (rows_in[1].astype(f32) + grad_x).astype(bf16)


def finish(source, pairs, cross, tokens, cotangent, gain, w_qkv, w_out):
    rows, width = tokens.shape
    n = len(pairs) + len(cross)
    out = jax.ShapeDtypeStruct((rows, width), bf16)
    return pl.pallas_call(
        finish_kernel,
        out_shape=[out, out],
        in_specs=[SMEM] + [ANY] * (n + 4) + [VMEM],
        out_specs=[VMEM] * 2,
        scratch_shapes=[
            pltpu.VMEM((n,) + cross[0].shape, bf16),
            pltpu.VMEM((4, width, width), bf16),
            pltpu.VMEM((4, rows, width), bf16),
            pltpu.VMEM((2, rows, width), bf16),
            pltpu.SemaphoreType.DMA((n + 6,)),
        ],
        compiler_params=params(60),
        cost_estimate=cost(32 * rows * width * width, 8 * width * width),
    )(source, *pairs, *cross, w_qkv, w_out, tokens, cotangent, gain)


def split3(table):
    first = table.astype(bf16)
    rest = table - first.astype(f32)
    second = rest.astype(bf16)
    third = (rest - second.astype(f32)).astype(bf16)
    return jnp.stack([first, second, third])


def rope_lookup(head_size):
    quarter = head_size // 4
    frequency = ROPE_BASE ** (-jnp.arange(quarter, dtype=f32) / quarter)

    def spread(limit, first):
        angles = jnp.arange(limit, dtype=f32)[:, None] * frequency
        cos, sin = jnp.cos(angles), jnp.sin(angles)
        none = jnp.zeros_like(cos)
        gap = jnp.zeros((limit, HALF - 2 * quarter), f32)
        pair = (lambda x: [x, none, gap]) if first else (lambda x: [none, x, gap])
        return jnp.concatenate(pair(cos) * 2 + pair(-sin) + pair(sin), axis=1)

    return split3(spread(ROW_LIMIT, True)), split3(spread(COL_LIMIT, False))


def gather(value, size):
    return [value] + [shift(value, OFFSETS[MIRROR[b]], size) for b in (1, 2, 3)]


def local(tokens, norm_gain, w_qkv, w_out, cotangent, segment, patch_row, patch_col):
    rows, width = tokens.shape
    size = lax.axis_size("seq")
    n_dp = lax.axis_size("dp")
    me = lax.axis_index("seq")
    head_size = width // HEADS
    own = HEADS // size * head_size
    padded = HEADS // size * LANES
    at = [((me // 2 + dz) % (size // 2)) * 2 + ((me % 2) ^ dc) for dz, dc in OFFSETS]
    at = jnp.stack(at).astype(jnp.int32)
    every = jnp.arange(size)
    steps = (every // 2 - me // 2) % (size // 2)
    source_of = jnp.where(steps == 0, 0, jnp.where(steps == size // 2 - 1, 1, steps + 1))
    source_of = (source_of + size // 2 * ((every % 2) ^ (me % 2))).astype(jnp.int32)

    payload = normalise(tokens, norm_gain, segment, patch_row, patch_col)
    mine = gather(payload, size)
    own_swap = shift(payload, (0, 1), size)
    cot_pair = jnp.stack([cotangent, shift(cotangent, (0, 1), size)])
    blocks = mine + [own_swap] + [shift(m, (0, 1), size) for m in mine[1:]]
    gm = grad_mixed_blocks(cotangent, w_out, size)
    gm = lax.all_to_all(gm, "seq", split_axis=0, concat_axis=0, tiled=True)

    lane = jnp.arange(padded)
    within = lane % HALF
    source = (lane // LANES) * head_size + (lane % LANES) // HALF * (head_size // 2) + within
    used = within < head_size // 2
    pick = ((source[:, None] == jnp.arange(own)[None, :]) & used[:, None]).astype(bf16)
    expand = ((source[None, :] == jnp.arange(own)[:, None]) & used[None, :]).astype(bf16)
    spread = ((source + me * own)[None, :] == jnp.arange(width)[:, None]) & used[None, :]
    spread = spread.astype(bf16)
    w_own = jnp.concatenate(
        [dot_nn(w_qkv[:, t * width : (t + 1) * width], spread).astype(bf16) for t in range(3)],
        axis=1,
    )
    table_r, table_c = rope_lookup(head_size)

    chunk = width // n_dp
    out_rows = chunk // size
    half_rows = own // 2
    row = jnp.arange(width // 2)
    moved_from = (row % chunk) // out_rows * half_rows + row // chunk * out_rows + row % out_rows
    move = (moved_from[:, None] == row[None, :]).astype(bf16)
    cot_pair, cot, _ = lax.optimization_barrier((cot_pair, cotangent, (mine[1:], own_swap)))
    cots = [cot_pair] + [shift(cot_pair, OFFSETS[MIRROR[b]], size) for b in (1, 2)]
    cots.append(shift(cot, OFFSETS[MIRROR[3]], size))
    w_own, move = lax.optimization_barrier((w_own, move))
    *attended, term_qkv, mixed = attend(at, blocks, gm, w_own, table_r, table_c, pick, expand)
    cots, attended = lax.optimization_barrier((cots, attended))
    cots.append(shift(cots[3], (0, 1), size))

    pairs = [attended[0]] + [None] * 3
    for b in (1, 2, 3):
        pairs[MIRROR[b]] = shift(attended[b], OFFSETS[b], size)

    terms = weight_terms(mixed, term_qkv, move, cots, n_dp)
    first = (lax.axis_index("dp") * size + me) * out_rows
    first, _ = lax.optimization_barrier((first, terms))
    pairs, _ = lax.optimization_barrier((pairs, terms))
    w_rows = lax.dynamic_slice(w_qkv, (first, 0), (out_rows, 3 * width)).astype(f32)
    gain_rows = lax.dynamic_slice(norm_gain, (first,), (out_rows,))
    cross = [shift(pair[1], (0, 1), size) for pair in pairs]
    terms = lax.all_to_all(terms, "dp", split_axis=0, concat_axis=0, tiled=True)
    result, grad_tokens = finish(
        source_of, pairs, cross, tokens, cotangent, norm_gain, w_qkv, w_out
    )

    factor = float(rows * size * n_dp) ** (-0.5)
    part_qkv, part_out = sum_terms(terms, size, own, factor)
    part_qkv = lax.all_to_all(part_qkv, "seq", split_axis=0, concat_axis=0, tiled=True)
    pairs = [(j * size + s, s * n_dp + j) for j in range(n_dp) for s in range(size)]
    grad_out = lax.ppermute(part_out, ("dp", "seq"), pairs)
    grad_qkv, grad_gain = place(part_qkv, w_rows, gain_rows)
    return (result, grad_tokens, grad_qkv, grad_out, grad_gain)


def solution(mesh):
    both = P(("dp", "seq"), None)
    flat = P(("dp", "seq"))
    return jax.shard_map(
        local,
        mesh=mesh,
        in_specs=(both, P(), P(), P(), both, flat, flat, flat),
        out_specs=(both, both, both, both, flat),
        check_vma=False,
    )
```
